256 devices in a mesh: dp: 32 (over y, x, core), ctx: 8 (over z).
Axes of the slice: x: 4, y: 4, z: 8, core: 2. Of those that a mesh axis runs over, the one named last changes fastest.
Arguments:
- queries: bfloat16 [32, 1024, 4096], P('dp', 'ctx'), may hold values from -128 to 128
- key_heads: bfloat16 [32, 1024, 1024], P('dp', 'ctx'), may hold values from -4 to 4
- value_heads: bfloat16 [32, 1024, 1024], P('dp', 'ctx'), may hold values from -6 to 6
- out_grad: bfloat16 [32, 1024, 4096], P('dp', 'ctx'), may hold values from -6 to 6
- routes: int32 [32, 1024], P('dp', 'ctx'), may hold values from 0 to 31, as said below
- doc_lengths: int32 [32, 8], P('dp'), may hold values from 1 to 512, 1024 in all within a row
Outputs:
- query_grad: bfloat16 [32, 1024, 4096], P('dp', 'ctx')
- key_grad: bfloat16 [32, 1024, 1024], P('dp', 'ctx')
- value_grad: bfloat16 [32, 1024, 1024], P('dp', 'ctx')
The draws below stay inside these ranges and needn't reach their ends.
Inputs may be any that keep to these rules, and one draw needn't show every extreme that they name: `routes`: each block of 128 loader positions c * 128 to (c + 1) * 128 - 1 of a loader sequence sends its tokens in contiguous runs, at most 8 of them to any one balanced sequence, and some block sends exactly 8 to one; every balanced sequence receives exactly 128 tokens from the blocks of each c.
All inputs are finite; a program needn't handle non-finite values.
Results may differ from the reference program's by a relative error of at most 0.027.
Values may be sent and summed in bfloat16 or wider, within the bound.
No kernel may reach another device: no remote copies, remote signals or barrier semaphores. Data moves between devices by JAX's collectives and lax.ppermute only.
A program may use at most 128 MiB of HBM per device.

```python
import math
import jax
import jax.numpy as jnp
import numpy as np
from jax import lax

QUERY_HEADS = 32
KEY_VALUE_HEADS = 8
HEAD_SIZE = 128
TOK_DEV = 128
NDOC = 8
QW = 4096
KW = 1024
PACKED_TOKENS = 1024
PACKED_COUNT = 32
N_CTX = 8


def draw_queries(key, part):
    key = jax.random.fold_in(key, 3)
    value_rows = jnp.clip(jax.random.normal(key, (PACKED_COUNT, PACKED_TOKENS, QUERY_HEADS, HEAD_SIZE), jnp.float32), -4.0, 4.0)
    return value_rows.reshape(PACKED_COUNT, PACKED_TOKENS, QUERY_HEADS * HEAD_SIZE).astype(jnp.bfloat16)


def draw_key_heads(key, part):
    key = jax.random.fold_in(key, 5)
    value_rows = jnp.clip(jax.random.normal(key, (PACKED_COUNT, PACKED_TOKENS, KEY_VALUE_HEADS, HEAD_SIZE), jnp.float32), -4.0, 4.0)
    return value_rows.reshape(PACKED_COUNT, PACKED_TOKENS, KEY_VALUE_HEADS * HEAD_SIZE).astype(jnp.bfloat16)


def draw_routes(key, part):
    key = jax.random.fold_in(key, 11)
    first_entry, second, third, fourth = jax.random.split(key, 4)
    half = TOK_DEV // PACKED_COUNT // 2
    base = jax.random.randint(first_entry, (N_CTX, PACKED_COUNT, PACKED_COUNT), 0, half + 1)
    corner_row = jax.random.randint(second, (N_CTX,), 0, PACKED_COUNT)
    corner_col = jax.random.randint(third, (N_CTX,), 0, PACKED_COUNT)
    indices = jnp.arange(PACKED_COUNT, dtype=jnp.int32)
    row_first = indices[None, :, None] == corner_row[:, None, None]
    row_second = indices[None, :, None] == (corner_row[:, None, None] + 1) % PACKED_COUNT
    col_first = indices[None, None, :] == corner_col[:, None, None]
    col_second = indices[None, None, :] == (corner_col[:, None, None] + 1) % PACKED_COUNT
    base = jnp.where(row_first & col_first | row_second & col_second, half, base)
    base = jnp.where(row_first & col_second | row_second & col_first, 0, base)
    shifted = jnp.roll(base, -1, axis=1)
    change = base - jnp.roll(base, -1, axis=2) - shifted + jnp.roll(shifted, -1, axis=2)
    counts = 2 * half + change
    perm_keys = jax.random.split(fourth, N_CTX * PACKED_COUNT)
    orders = jax.vmap(lambda single: jax.random.permutation(single, PACKED_COUNT))(perm_keys).reshape(N_CTX, PACKED_COUNT, PACKED_COUNT).astype(jnp.int32)
    ordered = jnp.take_along_axis(counts, orders, axis=2)
    run_ends = jnp.cumsum(ordered, axis=2)
    places = jnp.arange(TOK_DEV, dtype=jnp.int32)
    run_index = jnp.sum((places[None, None, :, None] >= run_ends[:, :, None, :]).astype(jnp.int32), axis=3)
    targets = jnp.take_along_axis(orders, run_index, axis=2)
    return targets.transpose(1, 0, 2).reshape(PACKED_COUNT, PACKED_TOKENS).astype(jnp.int32)


def block_levels(own_key, dims, shards, low, high):
    level = 1.0
    for dim, shards_of in shards:
        heights = jax.random.uniform(jax.random.fold_in(jax.random.fold_in(own_key, 6), dim), (shards_of,), jnp.float32, low / len(shards), high / len(shards))
        level = level * jnp.repeat(jnp.exp(heights), dims[dim] // shards_of).reshape((-1,) + (1,) * (len(dims) - 1 - dim))
    return level


def length_profile(amount, total, reach, skew):
    portions = [(1 << 20) // math.isqrt(grade ** skew) + 1 for grade in range(2, amount + 1)]
    rest, given = total - reach - (amount - 1), [1] * (amount - 1)
    while rest > 0:
        movable = [i for i in range(amount - 1) if given[i] < reach]
        whole, budget = sum([portions[i] for i in movable]), rest
        for i in movable:
            more = min(reach - given[i], max(1, budget * portions[i] // whole), rest)
            given[i] = given[i] + more
            rest = rest - more
    return np.array([reach] + given)


def uneven(stream_key, amount, total, reach, lean):
    if amount == 2:
        one = jax.random.randint(stream_key, (), max(1, total - reach), min(reach, total - 1) + 1)
        return jnp.stack([one, total - one])
    tallies = jnp.asarray(length_profile(amount, total, reach, lean), jnp.int32)
    twos = (amount - 1) // 2
    donor, receiver = tallies[1:1 + 2 * twos:2], tallies[2:2 + 2 * twos:2]
    margin = jnp.minimum(donor - 1, reach - receiver)
    moved = jax.random.randint(jax.random.fold_in(stream_key, 1), (twos,), 0, 1 << 20) % (margin + 1)
    tallies = tallies.at[1:1 + 2 * twos:2].set(donor - moved).at[2:2 + 2 * twos:2].set(receiver + moved)
    return tallies[jax.random.permutation(jax.random.fold_in(stream_key, 2), amount)]


def gaussian(key, shape, deviation, bound, cuts=(), held_as=jnp.bfloat16):
    result = jax.random.normal(key, shape, jnp.float32) * deviation
    if len(cuts) > 0:
        result = block_levels(key, shape, cuts, -0.22, 0.18) * result
    return jnp.clip(result, min=-bound, max=bound).astype(held_as)


def setup_inputs(seed: int = 0) -> dict:
    arg_keys = jax.random.split(jax.random.key(seed), 7)
    return {
        "queries": draw_queries(jax.random.fold_in(arg_keys[6], 71), 0),
        "key_heads": draw_key_heads(jax.random.fold_in(arg_keys[6], 71), 0),
        "value_heads": gaussian(arg_keys[2], (PACKED_COUNT, PACKED_TOKENS, KW), 1.0, 6.0, ((0, 32), (1, 8))),
        "out_grad": gaussian(arg_keys[3], (PACKED_COUNT, PACKED_TOKENS, QW), 1.0, 6.0, ((0, 32), (1, 8))),
        "routes": draw_routes(jax.random.fold_in(arg_keys[6], 71), 0),
        "doc_lengths": jax.vmap(lambda own: uneven(own, NDOC, PACKED_TOKENS, PACKED_TOKENS // 2, 2))(jax.random.split(arg_keys[5], PACKED_COUNT)).reshape((PACKED_COUNT, NDOC)).astype(jnp.int32),
    }


def segments(positions, lengths):
    run_ends = jnp.cumsum(lengths)
    return lax.optimization_barrier(jnp.sum((positions[:, None] >= run_ends[None, :]).astype(jnp.int32), axis=1))

def attend(query_block, key_block, value_block, grad_block, query_seg, key_seg, query_pos, key_pos):
    factor = 1.0 / math.sqrt(query_block.shape[-1])
    query_wide = query_block.astype(jnp.float32)
    key_wide = key_block.astype(jnp.float32)
    value_wide = value_block.astype(jnp.float32)
    grad_wide = grad_block.astype(jnp.float32)
    scores = jnp.einsum('rge,ke->grk', query_wide, key_wide) * factor
    allowed = (key_pos[None, :] <= query_pos[:, None]) & (key_seg[None, :] == query_seg[:, None])
    scores = jnp.where(allowed[None], scores, -1e+30)
    row_max = lax.optimization_barrier(jnp.max(scores, axis=2, keepdims=True))
    weights = jnp.exp(scores - row_max)
    probability = weights / lax.optimization_barrier(jnp.sum(weights, axis=2, keepdims=True))
    rounded_probs = probability.astype(jnp.bfloat16)
    attended = jnp.einsum('grk,ke->rge', rounded_probs.astype(jnp.float32), value_wide).astype(jnp.bfloat16)
    row_delta = jnp.transpose(lax.optimization_barrier(jnp.sum(grad_wide * attended.astype(jnp.float32), axis=2)))
    prob_grad = jnp.einsum('rge,ke->grk', grad_wide, value_wide)
    score_grad = (probability * (prob_grad - row_delta[:, :, None])).astype(jnp.bfloat16)
    score_wide = score_grad.astype(jnp.float32)
    query_grad = (jnp.einsum('grk,ke->rge', score_wide, key_wide) * factor).astype(jnp.bfloat16)
    key_grad = jnp.einsum('grk,rge->ke', score_wide, query_wide) * factor
    value_grad = jnp.einsum('grk,rge->ke', rounded_probs.astype(jnp.float32), grad_wide)
    return (query_grad, key_grad, value_grad)

def one_sequence(inputs):
    queries, key_heads, value_heads, out_grad, lengths = inputs
    positions = jnp.arange(PACKED_TOKENS, dtype=jnp.int32)
    doc_ids = segments(positions, lengths)
    query_group = QUERY_HEADS // KEY_VALUE_HEADS
    query_parts, key_parts, value_parts = ([], [], [])
    for head_position in range(KEY_VALUE_HEADS):
        query_cols = queries[:, head_position * query_group * HEAD_SIZE:(head_position + 1) * query_group * HEAD_SIZE].reshape(PACKED_TOKENS, query_group, HEAD_SIZE)
        grad_cols = out_grad[:, head_position * query_group * HEAD_SIZE:(head_position + 1) * query_group * HEAD_SIZE].reshape(PACKED_TOKENS, query_group, HEAD_SIZE)
        key_cols = key_heads[:, head_position * HEAD_SIZE:(head_position + 1) * HEAD_SIZE]
        value_cols = value_heads[:, head_position * HEAD_SIZE:(head_position + 1) * HEAD_SIZE]
        query_part, key_part, value_part = attend(query_cols, key_cols, value_cols, grad_cols, doc_ids, doc_ids, positions, positions)
        query_parts.append(query_part.reshape(PACKED_TOKENS, query_group * HEAD_SIZE))
        key_parts.append(key_part.astype(jnp.bfloat16))
        value_parts.append(value_part.astype(jnp.bfloat16))
    return (jnp.concatenate(query_parts, axis=1), jnp.concatenate(key_parts, axis=1), jnp.concatenate(value_parts, axis=1))

def reference(queries, key_heads, value_heads, out_grad, routes, doc_lengths):
    columns = routes.reshape(PACKED_COUNT, N_CTX, TOK_DEV).transpose(1, 0, 2).reshape(N_CTX, PACKED_COUNT * TOK_DEV)
    onehot = (columns[:, :, None] == jnp.arange(PACKED_COUNT, dtype=jnp.int32)[None, None, :]).astype(jnp.int32)
    earlier = jnp.cumsum(onehot, axis=1) - onehot
    rank = lax.optimization_barrier(jnp.sum(earlier * onehot, axis=2))
    rank = rank.reshape(N_CTX, PACKED_COUNT, TOK_DEV).transpose(1, 0, 2).reshape(PACKED_COUNT, PACKED_TOKENS)
    column_start = (jnp.arange(PACKED_TOKENS, dtype=jnp.int32) // TOK_DEV * TOK_DEV)[None, :]
    flat_target = (routes * PACKED_TOKENS + column_start + rank).reshape(PACKED_COUNT * PACKED_TOKENS).astype(jnp.int32)
    inverse = jnp.zeros((PACKED_COUNT * PACKED_TOKENS,), jnp.int32).at[flat_target].set(jnp.arange(PACKED_COUNT * PACKED_TOKENS, dtype=jnp.int32))

    def to_balanced(array):
        return jnp.take(array.reshape(PACKED_COUNT * PACKED_TOKENS, -1), inverse, axis=0).reshape(PACKED_COUNT, PACKED_TOKENS, -1)

    def to_loader(array):
        return jnp.take(array.reshape(PACKED_COUNT * PACKED_TOKENS, -1), flat_target, axis=0).reshape(PACKED_COUNT, PACKED_TOKENS, -1)
    results = lax.map(one_sequence, (to_balanced(queries), to_balanced(key_heads), to_balanced(value_heads), to_balanced(out_grad), doc_lengths))
    return (to_loader(results[0]), to_loader(results[1]), to_loader(results[2]))
```

```python
import functools
import math

import jax
import jax.numpy as jnp
from jax import lax
from jax.experimental import pallas as pl
from jax.experimental.pallas import tpu as pltpu
from jax.sharding import PartitionSpec as P

GROUPS = 8
GQ = 4
D = 128
T = 128
NDOC = 8
CAP = 8
S_DP = 32
SLOTS = S_DP * CAP
SEQ = GROUPS * T
FW = (1 + GQ) * D
BW = 3 * D
MARK = 1e30
BF = jnp.bfloat16
F32 = jnp.float32
NEG = -1e30
WINDOW = 5


def mm(a, b):
    return jnp.dot(a, b, preferred_element_type=F32)


def mm_nt(a, b):
    return lax.dot_general(a, b, (((1,), (1,)), ((), ())), preferred_element_type=F32)


def iota(shape, dim):
    return lax.broadcasted_iota(jnp.int32, shape, dim)


def ones_where(cond):
    return jnp.where(cond, 1.0, 0.0).astype(F32)


def rows_and_columns(route_rows):
    eye = ones_where(iota((T, T), 0) == iota((T, T), 1)).astype(BF)
    route_cols = mm_nt(eye, route_rows.astype(BF))
    same = route_rows == route_cols
    lane_rank = jnp.sum(ones_where(same & (iota((T, T), 0) < iota((T, T), 1))), axis=0, keepdims=True)
    sub_rank = jnp.sum(ones_where(same & (iota((T, T), 1) < iota((T, T), 0))), axis=1, keepdims=True)
    return lane_rank, route_cols, sub_rank


def split_kernel(routes_ref, v_ref, g_ref, *outs):
    me = lax.axis_index("ctx")
    for o, out in enumerate(outs):
        to = lax.rem(me + o, GROUPS)
        out[0:T, 0:D] = v_ref[:, pl.ds(pl.multiple_of(to * D, D), D)]
        out[0:T, D:FW] = g_ref[:, pl.ds(pl.multiple_of(to * GQ * D, D), GQ * D)]
        out[T : T + 16, 0:T] = jnp.broadcast_to(routes_ref[...].astype(F32), (16, T)).astype(BF)
        out[T : T + 16, T:FW] = jnp.zeros((16, FW - T), BF)


def pack_a_kernel(routes_ref, k_ref, q_ref, out):
    route_rows = jnp.broadcast_to(routes_ref[...].astype(F32), (T, T))
    lane_rank, _, _ = rows_and_columns(route_rows)
    slot = (route_rows[0:1, :] * CAP + lane_rank).astype(jnp.int32)
    onehot_f = ones_where(iota((SLOTS, T), 0) == slot)
    used = jnp.sum(onehot_f, axis=1, keepdims=True)
    onehot = onehot_f.astype(BF)
    for g in range(GROUPS):
        keys = mm(onehot, k_ref[:, g * D : (g + 1) * D])
        if g == 0:
            keys = jnp.where(used > 0.5, keys, MARK)
        out[:, g * FW : g * FW + D] = keys.astype(BF)
        out[:, g * FW + D : (g + 1) * FW] = mm(onehot, q_ref[:, g * GQ * D : (g + 1) * GQ * D]).astype(BF)


def unpack_a_kernel(r_ref, m_ref, *outs):
    me = lax.axis_index("ctx")
    flags = ones_where(r_ref[:, 0:D].astype(F32) < 0.5 * MARK)
    lower = ones_where(iota((SLOTS, SLOTS), 1) < iota((SLOTS, SLOTS), 0)).astype(BF)
    upper = ones_where(iota((SLOTS, SLOTS), 0) < iota((SLOTS, SLOTS), 1)).astype(BF)
    flags_b = flags.astype(BF)
    place = mm(lower, flags_b)
    hit = (place == iota((SLOTS, T), 1).astype(F32)) & (flags > 0.5)
    m_ref[...] = ones_where(hit).astype(BF)
    first = ones_where(iota((T, D), 1) == 0).astype(BF)
    flags_t = mm_nt(first, flags_b)
    place_t = mm(flags_t.astype(BF), upper)
    hit_t = (place_t == iota((T, SLOTS), 0).astype(F32)) & (flags_t > 0.5)
    pick = ones_where(hit_t).astype(BF)
    for o, out in enumerate(outs):
        to = lax.rem(me + o, GROUPS)
        out[...] = mm(pick, r_ref[:, pl.ds(pl.multiple_of(to * FW, D), FW)]).astype(BF)


def pack_b_kernel(*refs):
    blocks, (out, route_out), (rows,) = refs[:GROUPS], refs[GROUPS : GROUPS + 2], refs[GROUPS + 2 :]
    me = lax.axis_index("ctx")
    for o, block in enumerate(blocks):
        c = lax.rem(me - o + GROUPS, GROUPS)
        rows[pl.ds(pl.multiple_of(c * T, T), T), :] = block[0:T, :]
        route_out[pl.ds(pl.multiple_of(c * 8, 8), 8), :] = block[T : T + 16, 0:T].astype(F32)[0:8, :]
    for pair in range(GROUPS // 2):
        slots = []
        for low in range(2):
            c = 2 * pair + low
            route_rows = jnp.broadcast_to(route_out[8 * c : 8 * c + 1, :], (T, T))
            lane_rank, _, _ = rows_and_columns(route_rows)
            slots.append(route_rows[0:1, :] * (2 * CAP) + low * CAP + lane_rank)
        slot = jnp.concatenate(slots, axis=1).astype(jnp.int32)
        onehot_f = ones_where(iota((2 * SLOTS, 2 * T), 0) == slot)
        used = jnp.sum(onehot_f, axis=1, keepdims=True)
        onehot = onehot_f.astype(BF)
        x = mm(onehot, rows[2 * T * pair : 2 * T * (pair + 1), :])
        out[:, 16 * pair : 16 * pair + 16, 0:D] = (
            jnp.where(used > 0.5, x[:, 0:D], MARK).astype(BF).reshape(S_DP, 16, D)
        )
        out[:, 16 * pair : 16 * pair + 16, D:FW] = x[:, D:FW].astype(BF).reshape(S_DP, 16, FW - D)


def attend_kernel(*refs):
    lengths_ref, a_blocks, r_ref = refs[0], refs[1 : 1 + GROUPS], refs[1 + GROUPS]
    outs, packed = refs[2 + GROUPS : 2 + 2 * GROUPS], refs[2 + 2 * GROUPS]
    ks, vs, kt, qs, gs, place_m, dk, dv, back, s_s, p_s, pb_s, db_s = refs[3 + 2 * GROUPS :]
    me = lax.axis_index("ctx")
    factor = 1.0 / math.sqrt(D)
    eye = ones_where(iota((T, T), 0) == iota((T, T), 1)).astype(BF)
    for o, block in enumerate(a_blocks):
        c = lax.rem(me - o + GROUPS, GROUPS)
        ks[pl.ds(pl.multiple_of(c * T, T), T), :] = block[:, 0:D]
        kt[:, pl.ds(pl.multiple_of(c * T, T), T)] = mm_nt(eye, block[:, 0:D]).astype(BF)
        for j in range(GQ):
            qs[c, j * T : (j + 1) * T, :] = block[:, D * (1 + j) : D * (2 + j)]
    two = 2 * SLOTS
    row_low = (iota((two, two), 0) // CAP) % 2
    col_low = (iota((two, two), 1) // CAP) % 2
    lower = ones_where((iota((two, two), 1) < iota((two, two), 0)) & (row_low == col_low)).astype(BF)
    upper = ones_where((iota((two, two), 0) < iota((two, two), 1)) & (row_low == col_low)).astype(BF)
    slot_low = ((iota((two, T), 0) // CAP) % 2).astype(F32)
    slot_low_t = ((iota((T, two), 1) // CAP) % 2).astype(F32)
    first = ones_where(iota((T, D), 1) == 0).astype(BF)
    for pair in range(GROUPS // 2):
        r = r_ref[:, 16 * pair : 16 * pair + 16, :].reshape(two, FW)
        flags = ones_where(r[:, 0:D].astype(F32) < 0.5 * MARK)
        flags_b = flags.astype(BF)
        place = mm(lower, flags_b)
        hit = (place == iota((two, T), 1).astype(F32)) & (flags > 0.5)
        for low in range(2):
            place_m[pair, :, low * T : (low + 1) * T] = ones_where(hit & (slot_low == low)).astype(BF)
        flags_t = mm_nt(first, flags_b)
        place_t = mm(flags_t.astype(BF), upper)
        hit_t = (place_t == iota((T, two), 0).astype(F32)) & (flags_t > 0.5)
        for low in range(2):
            c = 2 * pair + low
            x = mm(ones_where(hit_t & (slot_low_t == low)).astype(BF), r).astype(BF)
            vs[c * T : (c + 1) * T, :] = x[:, 0:D]
            for j in range(GQ):
                gs[c, j * T : (j + 1) * T, :] = x[:, D * (1 + j) : D * (2 + j)]
    dk[...] = jnp.zeros_like(dk)
    dv[...] = jnp.zeros_like(dv)
    ends = []
    total = jnp.int32(0)
    for d in range(NDOC):
        total = total + lengths_ref[0, d]
        ends.append(total)
    half = 2 * T

    def query_block(i, _):
        base = i * T
        q_pos = base + lax.rem(iota((1, half), 1), T)
        doc_start = jnp.zeros((1, half), jnp.int32)
        first_start = jnp.int32(0)
        for end in ends:
            doc_start = jnp.where(q_pos >= end, end, doc_start)
            first_start = jnp.where(base >= end, end, first_start)
        k_block = first_start // T

        def run(blocks):
            start = pl.multiple_of((i - (blocks - 1)) * T, T)
            width = blocks * T
            for h in range(2):
                lanes = slice(h * half, (h + 1) * half)
                q = qs[i, lanes, :]
                top = None
                for b in range(blocks):
                    s = mm_nt(ks[pl.ds(start + b * T, T), :], q) * (factor * math.log2(math.e))
                    k_pos = start + b * T + iota((T, half), 0)
                    keep = k_pos >= doc_start
                    if b == blocks - 1:
                        keep = keep & (k_pos <= q_pos)
                    s = jnp.where(keep, s, NEG)
                    s_s[b * T : (b + 1) * T, lanes] = s
                    high = jnp.max(s, axis=0, keepdims=True)
                    top = high if top is None else jnp.maximum(top, high)
                g = gs[i, lanes, :]
                row_total = jnp.zeros((1, half), F32)
                delta = jnp.zeros((1, half), F32)
                for b in range(blocks):
                    e = jnp.exp2(s_s[b * T : (b + 1) * T, lanes] - top)
                    pg = mm_nt(vs[pl.ds(start + b * T, T), :], g)
                    s_s[b * T : (b + 1) * T, lanes] = e
                    p_s[b * T : (b + 1) * T, lanes] = pg
                    row_total = row_total + jnp.sum(e, axis=0, keepdims=True)
                    delta = delta + jnp.sum(e * pg, axis=0, keepdims=True)
                inverse = 1.0 / row_total
                delta = delta * inverse
                for b in range(blocks):
                    p = s_s[b * T : (b + 1) * T, lanes] * inverse
                    pb_s[b * T : (b + 1) * T, lanes] = p.astype(BF)
                    db_s[b * T : (b + 1) * T, lanes] = (p * (p_s[b * T : (b + 1) * T, lanes] - delta)).astype(BF)
            window = pl.ds(start, width)
            dv[window, :] += mm(pb_s[0:width, :], gs[i])
            dk[window, :] += mm(db_s[0:width, :], qs[i])
            dq_t = (mm(kt[:, window], db_s[0:width, :]) * factor).astype(BF)
            for j in range(GQ):
                dq = mm_nt(eye, dq_t[:, j * T : (j + 1) * T]).astype(BF)
                back[pl.ds(pl.multiple_of(base, T), T), j * D : (j + 1) * D] = dq

        for blocks in range(1, WINDOW + 1):
            pl.when(i - k_block + 1 == blocks)(functools.partial(run, blocks))
        return 0

    lax.fori_loop(0, GROUPS, query_block, 0)
    for o, out in enumerate(outs):
        c = lax.rem(me + o, GROUPS)
        out[...] = back[pl.ds(pl.multiple_of(c * T, T), T), 0:BW]
    for pair in range(GROUPS // 2):
        rows = slice(pair * 2 * T, (pair + 1) * 2 * T)
        y = jnp.concatenate(
            [back[rows, BW : BW + D], (dk[rows, :] * factor).astype(BF), dv[rows, :].astype(BF)], axis=1
        )
        packed[:, 16 * pair : 16 * pair + 16, :] = mm(place_m[pair], y).astype(BF).reshape(S_DP, 16, BW)


def restore_b_kernel(r_ref, route_ref, *refs):
    outs, rows = refs[:GROUPS], refs[GROUPS]
    me = lax.axis_index("ctx")
    for pair in range(GROUPS // 2):
        r = r_ref[:, 16 * pair : 16 * pair + 16, :].reshape(2 * SLOTS, BW)
        for low in range(2):
            c = 2 * pair + low
            route_rows = jnp.broadcast_to(route_ref[8 * c : 8 * c + 1, :], (T, T))
            _, route_cols, sub_rank = rows_and_columns(route_rows)
            slot = (route_cols[:, 0:1] * (2 * CAP) + low * CAP + sub_rank).astype(jnp.int32)
            pick = ones_where(iota((T, 2 * SLOTS), 1) == slot).astype(BF)
            rows[c * T : (c + 1) * T, :] = mm(pick, r).astype(BF)
    for o, out in enumerate(outs):
        c = lax.rem(me + o, GROUPS)
        out[...] = rows[pl.ds(pl.multiple_of(c * T, T), T), :]


def pack_back_kernel(m_ref, *refs):
    blocks, out = refs[:GROUPS], refs[GROUPS]
    me = lax.axis_index("ctx")
    for o, block in enumerate(blocks):
        g = lax.rem(me - o + GROUPS, GROUPS)
        out[:, pl.ds(pl.multiple_of(g * BW, D), BW)] = mm(m_ref[...], block[...]).astype(BF)


def finish_kernel(routes_ref, r_ref, *refs):
    blocks, (dq, dk, dv) = refs[:GROUPS], refs[GROUPS:]
    me = lax.axis_index("ctx")
    route_rows = jnp.broadcast_to(routes_ref[...].astype(F32), (T, T))
    _, route_cols, sub_rank = rows_and_columns(route_rows)
    slot = (route_cols[:, 0:1] * CAP + sub_rank).astype(jnp.int32)
    pick = ones_where(iota((T, SLOTS), 1) == slot).astype(BF)
    for g in range(GROUPS):
        dq[:, g * GQ * D : g * GQ * D + BW] = mm(pick, r_ref[:, g * BW : (g + 1) * BW]).astype(BF)
    for o, block in enumerate(blocks):
        g = lax.rem(me - o + GROUPS, GROUPS)
        dq[:, pl.ds(pl.multiple_of(g * GQ * D + BW, D), D)] = block[:, 0:D]
        dk[:, pl.ds(pl.multiple_of(g * D, D), D)] = block[:, D : 2 * D]
        dv[:, pl.ds(pl.multiple_of(g * D, D), D)] = block[:, 2 * D : 3 * D]


def call(kernel, shapes, args, scratch=(), smem=0, flops=0):
    size = sum(math.prod(s.shape) * s.dtype.itemsize for s in (*shapes, *args))
    vmem, scalar = pl.BlockSpec(memory_space=pltpu.VMEM), pl.BlockSpec(memory_space=pltpu.SMEM)
    return pl.pallas_call(
        kernel,
        out_shape=list(shapes),
        in_specs=[scalar] * smem + [vmem] * (len(args) - smem),
        out_specs=[vmem] * len(shapes),
        scratch_shapes=list(scratch),
        compiler_params=pltpu.CompilerParams(vmem_limit_bytes=48 * 1024 * 1024),
        cost_estimate=pl.CostEstimate(flops=flops, bytes_accessed=size, transcendentals=0),
    )(*args)


def shape(*dims, dtype=BF):
    return jax.ShapeDtypeStruct(dims, dtype)


def swap(blocks):
    n = len(blocks)
    return [
        blocks[o] if o == 0 else lax.ppermute(blocks[o], "ctx", [(i, (i + o) % n) for i in range(n)])
        for o in range(n)
    ]


def exchange(packed):
    return lax.all_to_all(packed, "dp", split_axis=0, concat_axis=0, tiled=True)


def body(queries, key_heads, value_heads, out_grad, routes, doc_lengths):
    q, k, v, g = queries[0], key_heads[0], value_heads[0], out_grad[0]
    b_blocks = call(split_kernel, [shape(T + 16, FW)] * GROUPS, [routes, v, g])
    b_arrived = swap(b_blocks)
    (a_packed,) = call(
        pack_a_kernel, [shape(SLOTS, GROUPS * FW)], [routes, k, q], flops=2 * SLOTS * T * GROUPS * FW
    )
    a_arrived = exchange(a_packed.reshape(S_DP, CAP, GROUPS * FW)).reshape(SLOTS, GROUPS * FW)
    place, *a_blocks = call(
        unpack_a_kernel,
        [shape(SLOTS, T)] + [shape(T, FW)] * GROUPS,
        [a_arrived],
        flops=2 * SLOTS * T * GROUPS * FW,
    )
    a_blocks = swap(a_blocks)
    b_packed, every_route = call(
        pack_b_kernel,
        [shape(S_DP, GROUPS * CAP, FW), shape(GROUPS * 8, T, dtype=F32)],
        b_arrived,
        [pltpu.VMEM((SEQ, FW), BF)],
        flops=2 * 2 * SLOTS * SEQ * FW,
    )
    b_seq = exchange(b_packed)
    *dq_blocks, back_packed = call(
        attend_kernel,
        [shape(T, BW)] * GROUPS + [shape(S_DP, GROUPS * CAP, BW)],
        [doc_lengths, *a_blocks, b_seq],
        [
            pltpu.VMEM((SEQ, D), BF),
            pltpu.VMEM((SEQ, D), BF),
            pltpu.VMEM((D, SEQ), BF),
            pltpu.VMEM((GROUPS, GQ * T, D), BF),
            pltpu.VMEM((GROUPS, GQ * T, D), BF),
            pltpu.VMEM((GROUPS // 2, 2 * SLOTS, 2 * T), BF),
            pltpu.VMEM((SEQ, D), F32),
            pltpu.VMEM((SEQ, D), F32),
            pltpu.VMEM((SEQ, GQ * D), BF),
            pltpu.VMEM((WINDOW * T, GQ * T), F32),
            pltpu.VMEM((WINDOW * T, GQ * T), F32),
            pltpu.VMEM((WINDOW * T, GQ * T), BF),
            pltpu.VMEM((WINDOW * T, GQ * T), BF),
        ],
        smem=1,
        flops=5 * 2 * 24 * T * T * GQ * D,
    )
    dq_arrived = swap(dq_blocks)
    back_arrived = exchange(back_packed)
    rest_blocks = call(
        restore_b_kernel,
        [shape(T, BW)] * GROUPS,
        [back_arrived, every_route],
        [pltpu.VMEM((SEQ, BW), BF)],
        flops=2 * 2 * SLOTS * SEQ * BW,
    )
    rest_arrived = swap(rest_blocks)
    (dq_packed,) = call(
        pack_back_kernel, [shape(SLOTS, GROUPS * BW)], [place, *dq_arrived], flops=2 * SLOTS * T * GROUPS * BW
    )
    dq_back = exchange(dq_packed.reshape(S_DP, CAP, GROUPS * BW)).reshape(SLOTS, GROUPS * BW)
    dq, dk, dv = call(
        finish_kernel,
        [shape(T, GROUPS * GQ * D), shape(T, GROUPS * D), shape(T, GROUPS * D)],
        [routes, dq_back, *rest_arrived],
        flops=2 * SLOTS * T * GROUPS * BW,
    )
    return dq[None], dk[None], dv[None]


def solution(mesh):
    return jax.shard_map(
        body,
        mesh=mesh,
        in_specs=(
            P("dp", "ctx", None),
            P("dp", "ctx", None),
            P("dp", "ctx", None),
            P("dp", "ctx", None),
            P("dp", "ctx"),
            P("dp", None),
        ),
        out_specs=(P("dp", "ctx", None), P("dp", "ctx", None), P("dp", "ctx", None)),
        check_vma=False,
    )
```

```python
import functools
import math

import jax
import jax.numpy as jnp
from jax import lax
from jax.experimental import pallas as pl
from jax.experimental.pallas import tpu as pltpu
from jax.sharding import PartitionSpec as P

GROUPS = 8
GQ = 4
D = 128
T = 128
NDOC = 8
CAP = 8
S_DP = 32
SLOTS = S_DP * CAP
SEQ = GROUPS * T
FW = (1 + GQ) * D
BW = 3 * D
MARK = 1e30
BF = jnp.bfloat16
F32 = jnp.float32
NEG = -1e30
WINDOW = 5


def mm(a, b):
    return jnp.dot(a, b, preferred_element_type=F32)


def mm_nt(a, b):
    return lax.dot_general(a, b, (((1,), (1,)), ((), ())), preferred_element_type=F32)


def iota(shape, dim):
    return lax.broadcasted_iota(jnp.int32, shape, dim)


def ones_where(cond):
    return jnp.where(cond, 1.0, 0.0).astype(F32)


def rows_and_columns(route_rows):
    eye = ones_where(iota((T, T), 0) == iota((T, T), 1)).astype(BF)
    route_cols = mm_nt(eye, route_rows.astype(BF))
    same = route_rows == route_cols
    lane_rank = jnp.sum(ones_where(same & (iota((T, T), 0) < iota((T, T), 1))), axis=0, keepdims=True)
    sub_rank = jnp.sum(ones_where(same & (iota((T, T), 1) < iota((T, T), 0))), axis=1, keepdims=True)
    return lane_rank, route_cols, sub_rank


def split_kernel(routes_ref, k_ref, q_ref, *outs):
    me = lax.axis_index("ctx")
    for o, out in enumerate(outs):
        to = lax.rem(me + o, GROUPS)
        out[0:T, :] = k_ref[:, pl.ds(pl.multiple_of(to * D, D), D)]
        for j in range(GQ):
            out[(1 + j) * T : (2 + j) * T, :] = q_ref[:, pl.ds(pl.multiple_of(to * GQ * D + j * D, D), D)]
        out[(1 + GQ) * T : (1 + GQ) * T + 16, :] = jnp.broadcast_to(routes_ref[...].astype(F32), (16, T)).astype(BF)


def pack_a_kernel(routes_ref, v_hbm, g_hbm, out_hbm, v_ref, g_ref, out, in_sem, out_sem):
    copies = []
    for g in range(GROUPS):
        vs, gs = slice(g * D, (g + 1) * D), slice(g * GQ * D, (g + 1) * GQ * D)
        copies.append(
            (
                pltpu.make_async_copy(v_hbm.at[:, vs], v_ref.at[:, vs], in_sem.at[0, g]),
                pltpu.make_async_copy(g_hbm.at[:, gs], g_ref.at[:, gs], in_sem.at[1, g]),
            )
        )
        for copy in copies[-1]:
            copy.start()
    route_rows = jnp.broadcast_to(routes_ref[...].astype(F32), (T, T))
    lane_rank, _, _ = rows_and_columns(route_rows)
    slot = (route_rows[0:1, :] * CAP + lane_rank).astype(jnp.int32)
    onehot_f = ones_where(iota((SLOTS, T), 0) == slot)
    used = jnp.sum(onehot_f, axis=1, keepdims=True)
    onehot = onehot_f.astype(BF)
    sent = []
    for g in range(GROUPS):
        for copy in copies[g]:
            copy.wait()
        values = mm(onehot, v_ref[:, g * D : (g + 1) * D])
        if g == 0:
            values = jnp.where(used > 0.5, values, MARK)
        out[:, g * FW : g * FW + D] = values.astype(BF)
        out[:, g * FW + D : (g + 1) * FW] = mm(onehot, g_ref[:, g * GQ * D : (g + 1) * GQ * D]).astype(BF)
        lanes = slice(g * FW, (g + 1) * FW)
        sent.append(pltpu.make_async_copy(out.at[:, lanes], out_hbm.at[:, lanes], out_sem.at[g]))
        sent[-1].start()
    for copy in sent:
        copy.wait()


def unpack_a_kernel(r_ref, m_ref, *outs):
    me = lax.axis_index("ctx")
    flags = ones_where(r_ref[:, 0:D].astype(F32) < 0.5 * MARK)
    lower = ones_where(iota((SLOTS, SLOTS), 1) < iota((SLOTS, SLOTS), 0)).astype(BF)
    upper = ones_where(iota((SLOTS, SLOTS), 0) < iota((SLOTS, SLOTS), 1)).astype(BF)
    flags_b = flags.astype(BF)
    place = mm(lower, flags_b)
    hit = (place == iota((SLOTS, T), 1).astype(F32)) & (flags > 0.5)
    m_ref[...] = ones_where(hit).astype(BF)
    first = ones_where(iota((T, D), 1) == 0).astype(BF)
    flags_t = mm_nt(first, flags_b)
    place_t = mm(flags_t.astype(BF), upper)
    hit_t = (place_t == iota((T, SLOTS), 0).astype(F32)) & (flags_t > 0.5)
    pick = ones_where(hit_t).astype(BF)
    for o, out in enumerate(outs):
        to = lax.rem(me + o, GROUPS)
        out[...] = mm(pick, r_ref[:, pl.ds(pl.multiple_of(to * FW, D), FW)]).astype(BF)


def pack_b_kernel(*refs):
    blocks, (out_hbm, route_out), (rows, out, out_sem) = refs[:GROUPS], refs[GROUPS + 1 : GROUPS + 3], refs[GROUPS + 3 :]
    sent = []
    me = lax.axis_index("ctx")
    for o, block in enumerate(blocks):
        c = lax.rem(me - o + GROUPS, GROUPS)
        for j in range(1 + GQ):
            rows[pl.ds(pl.multiple_of(c * T, T), T), j * D : (j + 1) * D] = block[j * T : (j + 1) * T, :]
        route_out[pl.ds(pl.multiple_of(c * 8, 8), 8), :] = block[(1 + GQ) * T :, :].astype(F32)[0:8, :]
    for pair in range(GROUPS // 2):
        slots = []
        for low in range(2):
            c = 2 * pair + low
            route_rows = jnp.broadcast_to(route_out[8 * c : 8 * c + 1, :], (T, T))
            lane_rank, _, _ = rows_and_columns(route_rows)
            slots.append(route_rows[0:1, :] * (2 * CAP) + low * CAP + lane_rank)
        slot = jnp.concatenate(slots, axis=1).astype(jnp.int32)
        onehot_f = ones_where(iota((2 * SLOTS, 2 * T), 0) == slot)
        used = jnp.sum(onehot_f, axis=1, keepdims=True)
        onehot = onehot_f.astype(BF)
        x = mm(onehot, rows[2 * T * pair : 2 * T * (pair + 1), :])
        out[:, 16 * pair : 16 * pair + 16, 0:D] = (
            jnp.where(used > 0.5, x[:, 0:D], MARK).astype(BF).reshape(S_DP, 16, D)
        )
        out[:, 16 * pair : 16 * pair + 16, D:FW] = x[:, D:FW].astype(BF).reshape(S_DP, 16, FW - D)
        part = (slice(None), slice(16 * pair, 16 * pair + 16), slice(None))
        sent.append(pltpu.make_async_copy(out.at[part], out_hbm.at[part], out_sem.at[pair]))
        sent[-1].start()
    for copy in sent:
        copy.wait()


def ends_of(lengths_ref):
    ends = []
    total = jnp.int32(0)
    for d in range(NDOC):
        total = total + lengths_ref[0, d]
        ends.append(total)
    return ends


def by_window(ends, i, run):
    first_start = jnp.int32(0)
    for end in ends:
        first_start = jnp.where(i * T >= end, end, first_start)
    reach = i - first_start // T + 1
    for blocks in range(1, WINDOW + 1):
        pl.when(reach == blocks)(functools.partial(run, blocks))


def scores_kernel(lengths_ref, r_ref, place_m, ks, kt, qs, probs, s_s):
    eye = ones_where(iota((T, T), 0) == iota((T, T), 1)).astype(BF)
    two = 2 * SLOTS
    row_low = (iota((two, two), 0) // CAP) % 2
    col_low = (iota((two, two), 1) // CAP) % 2
    lower = ones_where((iota((two, two), 1) < iota((two, two), 0)) & (row_low == col_low)).astype(BF)
    upper = ones_where((iota((two, two), 0) < iota((two, two), 1)) & (row_low == col_low)).astype(BF)
    slot_low = ((iota((two, T), 0) // CAP) % 2).astype(F32)
    slot_low_t = ((iota((T, two), 1) // CAP) % 2).astype(F32)
    first = ones_where(iota((T, D), 1) == 0).astype(BF)
    for pair in range(GROUPS // 2):
        r = r_ref[:, 16 * pair : 16 * pair + 16, :].reshape(two, FW)
        flags = ones_where(r[:, 0:D].astype(F32) < 0.5 * MARK)
        flags_b = flags.astype(BF)
        place = mm(lower, flags_b)
        hit = (place == iota((two, T), 1).astype(F32)) & (flags > 0.5)
        for low in range(2):
            place_m[pair, :, low * T : (low + 1) * T] = ones_where(hit & (slot_low == low)).astype(BF)
        flags_t = mm_nt(first, flags_b)
        place_t = mm(flags_t.astype(BF), upper)
        hit_t = (place_t == iota((T, two), 0).astype(F32)) & (flags_t > 0.5)
        for low in range(2):
            c = 2 * pair + low
            x = mm(ones_where(hit_t & (slot_low_t == low)).astype(BF), r).astype(BF)
            ks[c * T : (c + 1) * T, :] = x[:, 0:D]
            kt[:, c * T : (c + 1) * T] = mm_nt(eye, x[:, 0:D]).astype(BF)
            for j in range(GQ):
                qs[c, j * T : (j + 1) * T, :] = x[:, D * (1 + j) : D * (2 + j)]
    ends = ends_of(lengths_ref)
    half = 2 * T
    scale = math.log2(math.e) / math.sqrt(D)

    def query_block(i, _):
        q_pos = i * T + lax.rem(iota((1, half), 1), T)
        doc_start = jnp.zeros((1, half), jnp.int32)
        for end in ends:
            doc_start = jnp.where(q_pos >= end, end, doc_start)

        def run(blocks):
            start = pl.multiple_of((i - (blocks - 1)) * T, T)
            for h in range(2):
                lanes = slice(h * half, (h + 1) * half)
                q = qs[i, lanes, :]
                top = None
                for b in range(blocks):
                    s = mm_nt(ks[pl.ds(start + b * T, T), :], q) * scale
                    k_pos = start + b * T + iota((T, half), 0)
                    keep = k_pos >= doc_start
                    if b == blocks - 1:
                        keep = keep & (k_pos <= q_pos)
                    s = jnp.where(keep, s, NEG)
                    s_s[b * T : (b + 1) * T, lanes] = s
                    high = jnp.max(s, axis=0, keepdims=True)
                    top = high if top is None else jnp.maximum(top, high)
                row_total = jnp.zeros((1, half), F32)
                for b in range(blocks):
                    e = jnp.exp2(s_s[b * T : (b + 1) * T, lanes] - top)
                    s_s[b * T : (b + 1) * T, lanes] = e
                    row_total = row_total + jnp.sum(e, axis=0, keepdims=True)
                inverse = 1.0 / row_total
                for b in range(blocks):
                    probs[i, b * T : (b + 1) * T, lanes] = (s_s[b * T : (b + 1) * T, lanes] * inverse).astype(BF)

        by_window(ends, i, run)
        return 0

    lax.fori_loop(0, GROUPS, query_block, 0)


def gather_rows(blocks, vs, gs):
    me = lax.axis_index("ctx")
    for o, block in enumerate(blocks):
        c = lax.rem(me - o + GROUPS, GROUPS)
        vs[pl.ds(pl.multiple_of(c * T, T), T), :] = block[:, 0:D]
        for j in range(GQ):
            gs[c, j * T : (j + 1) * T, :] = block[:, D * (1 + j) : D * (2 + j)]


def gradients(lengths_ref, kt, qs, probs, vs, gs, dk, dv, back, pg_s, db_s):
    eye = ones_where(iota((T, T), 0) == iota((T, T), 1)).astype(BF)
    factor = 1.0 / math.sqrt(D)
    ends = ends_of(lengths_ref)
    half = 2 * T

    def query_block(i, _):
        def run(blocks):
            start = pl.multiple_of((i - (blocks - 1)) * T, T)
            width = blocks * T
            window = pl.ds(start, width)
            for h in range(2):
                lanes = slice(h * half, (h + 1) * half)
                g = gs[i, lanes, :]
                delta = jnp.zeros((1, half), F32)
                for b in range(blocks):
                    rows = slice(b * T, (b + 1) * T)
                    pg = mm_nt(vs[pl.ds(start + b * T, T), :], g)
                    pg_s[rows, lanes] = pg
                    delta = delta + jnp.sum(probs[i, rows, lanes].astype(F32) * pg, axis=0, keepdims=True)
                for b in range(blocks):
                    rows = slice(b * T, (b + 1) * T)
                    db_s[rows, lanes] = (probs[i, rows, lanes].astype(F32) * (pg_s[rows, lanes] - delta)).astype(BF)
            dv[window, :] += mm(probs[i, 0:width, :], gs[i])
            dk[window, :] += mm(db_s[0:width, :], qs[i])
            dq_t = (mm(kt[:, window], db_s[0:width, :]) * factor).astype(BF)
            for j in range(GQ):
                dq = mm_nt(eye, dq_t[:, j * T : (j + 1) * T]).astype(BF)
                back[pl.ds(pl.multiple_of(i * T, T), T), j * D : (j + 1) * D] = dq

        by_window(ends, i, run)
        return 0

    lax.fori_loop(0, GROUPS, query_block, 0)


def grad_kernel(lengths_ref, kt, qs, probs, place_m, *refs):
    blocks, outs, packed = refs[:GROUPS], refs[GROUPS : 2 * GROUPS], refs[2 * GROUPS]
    dk, dv, vs, gs, back, pg_s, db_s = refs[2 * GROUPS + 1 :]
    me = lax.axis_index("ctx")
    gather_rows(blocks, vs, gs)
    dk[...] = jnp.zeros_like(dk)
    dv[...] = jnp.zeros_like(dv)
    gradients(lengths_ref, kt, qs, probs, vs, gs, dk, dv, back, pg_s, db_s)
    for o, out in enumerate(outs):
        c = lax.rem(me + o, GROUPS)
        out[...] = back[pl.ds(pl.multiple_of(c * T, T), T), 0:BW]
    factor = 1.0 / math.sqrt(D)
    for pair in range(GROUPS // 2):
        rows = slice(pair * 2 * T, (pair + 1) * 2 * T)
        y = jnp.concatenate(
            [back[rows, BW : BW + D], (dk[rows, :] * factor).astype(BF), dv[rows, :].astype(BF)], axis=1
        )
        packed[:, 16 * pair : 16 * pair + 16, :] = mm(place_m[pair], y).astype(BF).reshape(S_DP, 16, BW)


def restore_b_kernel(r_ref, route_ref, *refs):
    outs, rows = refs[:GROUPS], refs[GROUPS]
    me = lax.axis_index("ctx")
    for pair in range(GROUPS // 2):
        r = r_ref[:, 16 * pair : 16 * pair + 16, :].reshape(2 * SLOTS, BW)
        for low in range(2):
            c = 2 * pair + low
            route_rows = jnp.broadcast_to(route_ref[8 * c : 8 * c + 1, :], (T, T))
            _, route_cols, sub_rank = rows_and_columns(route_rows)
            slot = (route_cols[:, 0:1] * (2 * CAP) + low * CAP + sub_rank).astype(jnp.int32)
            pick = ones_where(iota((T, 2 * SLOTS), 1) == slot).astype(BF)
            rows[c * T : (c + 1) * T, :] = mm(pick, r).astype(BF)
    for o, out in enumerate(outs):
        c = lax.rem(me + o, GROUPS)
        out[...] = rows[pl.ds(pl.multiple_of(c * T, T), T), :]


def pack_back_kernel(m_ref, *refs):
    blocks, out = refs[:GROUPS], refs[GROUPS + 1]
    me = lax.axis_index("ctx")
    for o, block in enumerate(blocks):
        g = lax.rem(me - o + GROUPS, GROUPS)
        out[:, pl.ds(pl.multiple_of(g * BW, D), BW)] = mm(m_ref[...], block[...]).astype(BF)


def finish_kernel(routes_ref, r_ref, *refs):
    blocks, (dq, dk, dv) = refs[:GROUPS], refs[GROUPS:]
    me = lax.axis_index("ctx")
    route_rows = jnp.broadcast_to(routes_ref[...].astype(F32), (T, T))
    _, route_cols, sub_rank = rows_and_columns(route_rows)
    slot = (route_cols[:, 0:1] * CAP + sub_rank).astype(jnp.int32)
    pick = ones_where(iota((T, SLOTS), 1) == slot).astype(BF)
    for g in range(GROUPS):
        dq[:, g * GQ * D : g * GQ * D + BW] = mm(pick, r_ref[:, g * BW : (g + 1) * BW]).astype(BF)
    for o, block in enumerate(blocks):
        g = lax.rem(me - o + GROUPS, GROUPS)
        dq[:, pl.ds(pl.multiple_of(g * GQ * D + BW, D), D)] = block[:, 0:D]
        dk[:, pl.ds(pl.multiple_of(g * D, D), D)] = block[:, D : 2 * D]
        dv[:, pl.ds(pl.multiple_of(g * D, D), D)] = block[:, 2 * D : 3 * D]


def call(kernel, shapes, args, scratch=(), smem=0, hbm=(), vmem=32, flops=0):
    size = sum(math.prod(s.shape) * s.dtype.itemsize for s in (*shapes, *args))
    specs = [
        pl.BlockSpec(memory_space=pltpu.SMEM if i < smem else pltpu.HBM if i in hbm else pltpu.VMEM)
        for i in range(len(args) + len(shapes))
    ]
    return pl.pallas_call(
        kernel,
        out_shape=list(shapes),
        in_specs=specs[: len(args)],
        out_specs=specs[len(args) :],
        scratch_shapes=list(scratch),
        name=kernel.__name__,
        compiler_params=pltpu.CompilerParams(vmem_limit_bytes=vmem * 1024 * 1024),
        cost_estimate=pl.CostEstimate(flops=flops, bytes_accessed=size, transcendentals=0),
    )(*args)


def shape(*dims, dtype=BF):
    return jax.ShapeDtypeStruct(dims, dtype)


def swap(blocks):
    n = len(blocks)
    arrived = list(blocks)
    for o in (4, 3, 5, 2, 6, 1, 7):
        arrived[o] = lax.ppermute(blocks[o], "ctx", [(i, (i + o) % n) for i in range(n)])
    return arrived


def exchange(packed):
    return lax.all_to_all(packed, "dp", split_axis=0, concat_axis=0, tiled=True)


def body(queries, key_heads, value_heads, out_grad, routes, doc_lengths):
    q, k, v, g = queries[0], key_heads[0], value_heads[0], out_grad[0]
    b_blocks = call(split_kernel, [shape((1 + GQ) * T + 16, D)] * GROUPS, [routes, k, q])
    b_arrived = swap(b_blocks)
    (a_packed,) = call(
        pack_a_kernel,
        [shape(SLOTS, GROUPS * FW)],
        [routes, v, g],
        [
            pltpu.VMEM((T, GROUPS * D), BF),
            pltpu.VMEM((T, GROUPS * GQ * D), BF),
            pltpu.VMEM((SLOTS, GROUPS * FW), BF),
            pltpu.SemaphoreType.DMA((2, GROUPS)),
            pltpu.SemaphoreType.DMA((GROUPS,)),
        ],
        hbm=(1, 2, 3),
        vmem=60,
        flops=2 * SLOTS * T * GROUPS * FW,
    )
    a_arrived = exchange(a_packed.reshape(S_DP, CAP, GROUPS * FW)).reshape(SLOTS, GROUPS * FW)
    place, *a_blocks = call(
        unpack_a_kernel,
        [shape(SLOTS, T)] + [shape(T, FW)] * GROUPS,
        [a_arrived],
        flops=2 * SLOTS * T * GROUPS * FW,
    )
    a_blocks = swap(a_blocks)
    b_packed, every_route = call(
        pack_b_kernel,
        [shape(S_DP, GROUPS * CAP, FW), shape(GROUPS * 8, T, dtype=F32)],
        [*b_arrived, place],
        [
            pltpu.VMEM((SEQ, FW), BF),
            pltpu.VMEM((S_DP, GROUPS * CAP, FW), BF),
            pltpu.SemaphoreType.DMA((GROUPS // 2,)),
        ],
        hbm=(GROUPS, GROUPS + 1),
        flops=2 * 2 * SLOTS * SEQ * FW,
    )
    b_seq = exchange(b_packed)
    place_b, ks, kt, qs, probs = call(
        scores_kernel,
        [
            shape(GROUPS // 2, 2 * SLOTS, 2 * T),
            shape(SEQ, D),
            shape(D, SEQ),
            shape(GROUPS, GQ * T, D),
            shape(GROUPS, WINDOW * T, GQ * T),
        ],
        [doc_lengths, b_seq],
        [pltpu.VMEM((WINDOW * T, GQ * T), F32)],
        smem=1,
        flops=2 * 2 * SLOTS * SEQ * FW + 2 * 24 * T * T * GQ * D,
    )

    *dq_blocks, back_packed = call(
        grad_kernel,
        [shape(T, BW)] * GROUPS + [shape(S_DP, GROUPS * CAP, BW)],
        [doc_lengths, kt, qs, probs, place_b, *a_blocks],
        [
            pltpu.VMEM((SEQ, D), F32),
            pltpu.VMEM((SEQ, D), F32),
            pltpu.VMEM((SEQ, D), BF),
            pltpu.VMEM((GROUPS, GQ * T, D), BF),
            pltpu.VMEM((SEQ, GQ * D), BF),
            pltpu.VMEM((WINDOW * T, GQ * T), F32),
            pltpu.VMEM((WINDOW * T, GQ * T), BF),
        ],
        smem=1,
        flops=4 * 2 * 24 * T * T * GQ * D,
    )
    dq_arrived = swap(dq_blocks)
    back_arrived = exchange(back_packed)
    rest_blocks = call(
        restore_b_kernel,
        [shape(T, BW)] * GROUPS,
        [back_arrived, every_route],
        [pltpu.VMEM((SEQ, BW), BF)],
        flops=2 * 2 * SLOTS * SEQ * BW,
    )
    rest_arrived = swap(rest_blocks)
    (dq_packed,) = call(
        pack_back_kernel,
        [shape(SLOTS, GROUPS * BW)],
        [place, *dq_arrived, rest_blocks[0]],
        hbm=(1 + GROUPS,),
        flops=2 * SLOTS * T * GROUPS * BW,
    )
    dq_back = exchange(dq_packed.reshape(S_DP, CAP, GROUPS * BW)).reshape(SLOTS, GROUPS * BW)
    dq, dk, dv = call(
        finish_kernel,
        [shape(T, GROUPS * GQ * D), shape(T, GROUPS * D), shape(T, GROUPS * D)],
        [routes, dq_back, *rest_arrived],
        flops=2 * SLOTS * T * GROUPS * BW,
    )
    return dq[None], dk[None], dv[None]


def solution(mesh):
    return jax.shard_map(
        body,
        mesh=mesh,
        in_specs=(
            P("dp", "ctx", None),
            P("dp", "ctx", None),
            P("dp", "ctx", None),
            P("dp", "ctx", None),
            P("dp", "ctx"),
            P("dp", None),
        ),
        out_specs=(P("dp", "ctx", None), P("dp", "ctx", None), P("dp", "ctx", None)),
        check_vma=False,
    )
```

```python
import functools
import math

import jax
import jax.numpy as jnp
from jax import lax
from jax.experimental import pallas as pl
from jax.experimental.pallas import tpu as pltpu
from jax.sharding import PartitionSpec as P

GROUPS = 8
GQ = 4
D = 128
T = 128
NDOC = 8
CAP = 8
S_DP = 32
SLOTS = S_DP * CAP
SEQ = GROUPS * T
FW = (1 + GQ) * D
BW = 3 * D
MARK = 1e30
BF = jnp.bfloat16
F32 = jnp.float32
NEG = -1e30
ORDER = (0, 4, 3, 5, 2, 6, 1, 7)
WINDOW = 5


def mm(a, b):
    return jnp.dot(a, b, preferred_element_type=F32)


def mm_nt(a, b):
    return lax.dot_general(a, b, (((1,), (1,)), ((), ())), preferred_element_type=F32)


def iota(shape, dim):
    return lax.broadcasted_iota(jnp.int32, shape, dim)


def ones_where(cond):
    return jnp.where(cond, 1.0, 0.0).astype(F32)


def rows_and_columns(route_rows):
    eye = ones_where(iota((T, T), 0) == iota((T, T), 1)).astype(BF)
    route_cols = mm_nt(eye, route_rows.astype(BF))
    same = route_rows == route_cols
    lane_rank = jnp.sum(ones_where(same & (iota((T, T), 0) < iota((T, T), 1))), axis=0, keepdims=True)
    sub_rank = jnp.sum(ones_where(same & (iota((T, T), 1) < iota((T, T), 0))), axis=1, keepdims=True)
    return lane_rank, route_cols, sub_rank


def enter_kernel(routes_ref, k_hbm, q_hbm, v_hbm, g_hbm, *refs):
    outs, packed_hbm = refs[:GROUPS], refs[GROUPS]
    k_ref, q_ref, v_ref, g_ref, packed, route_tile, in_sem, out_sem, stack_sem = refs[GROUPS + 1 :]
    me = lax.axis_index("ctx")
    step = 2
    arriving, leaving = [], []
    stacking = (
        pltpu.make_async_copy(q_hbm, q_ref, in_sem.at[0, GROUPS // step]),
        pltpu.make_async_copy(k_hbm, k_ref, in_sem.at[1, GROUPS // step]),
    )
    for copy in stacking:
        copy.start()
    for n, g in enumerate(range(0, GROUPS, step)):
        vs, gs = slice(g * D, (g + step) * D), slice(g * GQ * D, (g + step) * GQ * D)
        pair = (
            pltpu.make_async_copy(v_hbm.at[:, vs], v_ref.at[:, vs], in_sem.at[0, n]),
            pltpu.make_async_copy(g_hbm.at[:, gs], g_ref.at[:, gs], in_sem.at[1, n]),
        )
        arriving.append(pair)
        for copy in pair:
            copy.start()
    route_tile[...] = jnp.broadcast_to(routes_ref[...].astype(F32), (16, T)).astype(BF)
    for copy in stacking:
        copy.wait()
    for n, (o, out) in enumerate(zip(ORDER, outs)):
        to = lax.rem(me + o, GROUPS)
        parts = [(k_ref.at[:, pl.ds(pl.multiple_of(to * D, D), D)], out.at[0:T, :])]
        for j in range(GQ):
            lanes = pl.ds(pl.multiple_of(to * GQ * D + j * D, D), D)
            parts.append((q_ref.at[:, lanes], out.at[(1 + j) * T : (2 + j) * T, :]))
        parts.append((route_tile, out.at[(1 + GQ) * T : (1 + GQ) * T + 16, :]))
        for m, (source, target) in enumerate(parts):
            leaving.append(pltpu.make_async_copy(source, target, stack_sem.at[n, m]))
            leaving[-1].start()
    route_rows = jnp.broadcast_to(routes_ref[...].astype(F32), (T, T))
    lane_rank, _, _ = rows_and_columns(route_rows)
    slot = (route_rows[0:1, :] * CAP + lane_rank).astype(jnp.int32)
    onehot = ones_where(iota((SLOTS, T), 0) == slot).astype(BF)
    unused = 1.0 - mm(onehot, jnp.ones((T, D), BF))
    for n, pair in enumerate(arriving):
        for copy in pair:
            copy.wait()
        for g in range(n * step, (n + 1) * step):
            values = mm(onehot, v_ref[:, g * D : (g + 1) * D])
            if g == 0:
                values = values + unused * MARK
            packed[:, g * FW : g * FW + D] = values.astype(BF)
            packed[:, g * FW + D : (g + 1) * FW] = mm(onehot, g_ref[:, g * GQ * D : (g + 1) * GQ * D]).astype(BF)
        lanes = slice(n * step * FW, (n + 1) * step * FW)
        leaving.append(pltpu.make_async_copy(packed.at[:, lanes], packed_hbm.at[:, lanes], out_sem.at[n]))
        leaving[-1].start()
    for copy in leaving:
        copy.wait()


def unpack_a_kernel(r_ref, m_ref, *outs):
    me = lax.axis_index("ctx")
    flags = ones_where(r_ref[:, 0:D].astype(F32) < 0.5 * MARK)
    lower = ones_where(iota((SLOTS, SLOTS), 1) < iota((SLOTS, SLOTS), 0)).astype(BF)
    flags_b = flags.astype(BF)
    place = mm(lower, flags_b)
    hit = (place == iota((SLOTS, T), 1).astype(F32)) & (flags > 0.5)
    m_ref[...] = ones_where(hit).astype(BF)
    first = ones_where(iota((T, D), 1) == 0).astype(BF)
    flags_t = mm_nt(first, flags_b)
    place_t = mm_nt(flags_t.astype(BF), lower)
    hit_t = (place_t == iota((T, SLOTS), 0).astype(F32)) & (flags_t > 0.5)
    pick = ones_where(hit_t).astype(BF)
    for o, out in zip(ORDER, outs):
        to = lax.rem(me + o, GROUPS)
        out[...] = mm(pick, r_ref[:, pl.ds(pl.multiple_of(to * FW, D), FW)]).astype(BF)


def pack_b_kernel(*refs):
    blocks, (out_hbm, route_out), (rows, out, out_sem) = refs[:GROUPS], refs[GROUPS + 1 : GROUPS + 3], refs[GROUPS + 3 :]
    sent = []
    me = lax.axis_index("ctx")
    for o, block in zip(ORDER, blocks):
        c = lax.rem(me - o + GROUPS, GROUPS)
        for j in range(1 + GQ):
            rows[pl.ds(pl.multiple_of(c * T, T), T), j * D : (j + 1) * D] = block[j * T : (j + 1) * T, :]
        route_out[pl.ds(pl.multiple_of(c * 8, 8), 8), :] = block[(1 + GQ) * T :, :].astype(F32)[0:8, :]
    for pair in range(GROUPS // 2):
        slots = []
        for low in range(2):
            c = 2 * pair + low
            route_rows = jnp.broadcast_to(route_out[8 * c : 8 * c + 1, :], (T, T))
            lane_rank, _, _ = rows_and_columns(route_rows)
            slots.append(route_rows[0:1, :] * (2 * CAP) + low * CAP + lane_rank)
        slot = jnp.concatenate(slots, axis=1).astype(jnp.int32)
        onehot = ones_where(iota((2 * SLOTS, 2 * T), 0) == slot).astype(BF)
        unused = 1.0 - mm(onehot, jnp.ones((2 * T, D), BF))
        x = mm(onehot, rows[2 * T * pair : 2 * T * (pair + 1), :])
        out[:, 16 * pair : 16 * pair + 16, 0:D] = (
            (x[:, 0:D] + unused * MARK).astype(BF).reshape(S_DP, 16, D)
        )
        out[:, 16 * pair : 16 * pair + 16, D:FW] = x[:, D:FW].astype(BF).reshape(S_DP, 16, FW - D)
        part = (slice(None), slice(16 * pair, 16 * pair + 16), slice(None))
        sent.append(pltpu.make_async_copy(out.at[part], out_hbm.at[part], out_sem.at[pair]))
        sent[-1].start()
    for copy in sent:
        copy.wait()


def ends_of(lengths_ref):
    ends = []
    total = jnp.int32(0)
    for d in range(NDOC):
        total = total + lengths_ref[0, d]
        ends.append(total)
    return ends


def by_window(ends, i, run):
    first_start = jnp.int32(0)
    for end in ends:
        first_start = jnp.where(i * T >= end, end, first_start)
    reach = i - first_start // T + 1
    for blocks in range(1, WINDOW + 1):
        pl.when(reach == blocks)(functools.partial(run, blocks))


def scores_kernel(lengths_ref, r_ref, place_m, ks, kt, qs, probs, s_s):
    eye = ones_where(iota((T, T), 0) == iota((T, T), 1)).astype(BF)
    two = 2 * SLOTS
    row, col = iota((two, two), 0), iota((two, two), 1)
    lower = ones_where((col < row) & (((row ^ col) & CAP) == 0)).astype(BF)
    slot_low = iota((two, T), 0) & CAP
    slot_low_t = iota((T, two), 1) & CAP
    first = ones_where(iota((T, D), 1) == 0).astype(BF)
    for pair in range(GROUPS // 2):
        r = r_ref[:, 16 * pair : 16 * pair + 16, :].reshape(two, FW)
        flags = ones_where(r[:, 0:D].astype(F32) < 0.5 * MARK)
        flags_b = flags.astype(BF)
        place = mm(lower, flags_b)
        hit = (place == iota((two, T), 1).astype(F32)) & (flags > 0.5)
        for low in range(2):
            place_m[pair, :, low * T : (low + 1) * T] = ones_where(hit & (slot_low == low * CAP)).astype(BF)
        flags_t = mm_nt(first, flags_b)
        place_t = mm_nt(flags_t.astype(BF), lower)
        hit_t = (place_t == iota((T, two), 0).astype(F32)) & (flags_t > 0.5)
        for low in range(2):
            c = 2 * pair + low
            x = mm(ones_where(hit_t & (slot_low_t == low * CAP)).astype(BF), r).astype(BF)
            ks[c * T : (c + 1) * T, :] = x[:, 0:D]
            kt[:, c * T : (c + 1) * T] = mm_nt(eye, x[:, 0:D]).astype(BF)
            for j in range(GQ):
                qs[c, j * T : (j + 1) * T, :] = x[:, D * (1 + j) : D * (2 + j)]
    ends = ends_of(lengths_ref)
    half = 2 * T
    scale = math.log2(math.e) / math.sqrt(D)

    def query_block(i, _):
        q_pos = i * T + lax.rem(iota((1, half), 1), T)
        doc_start = jnp.zeros((1, half), jnp.int32)
        for end in ends:
            doc_start = jnp.where(q_pos >= end, end, doc_start)

        def run(blocks):
            start = pl.multiple_of((i - (blocks - 1)) * T, T)
            for h in range(2):
                lanes = slice(h * half, (h + 1) * half)
                q = qs[i, lanes, :]
                top = None
                for b in range(blocks):
                    s = mm_nt(ks[pl.ds(start + b * T, T), :], q) * scale
                    k_pos = start + b * T + iota((T, half), 0)
                    keep = k_pos >= doc_start
                    if b == blocks - 1:
                        keep = keep & (k_pos <= q_pos)
                    s = jnp.where(keep, s, NEG)
                    s_s[b * T : (b + 1) * T, lanes] = s
                    high = jnp.max(s, axis=0, keepdims=True)
                    top = high if top is None else jnp.maximum(top, high)
                row_total = jnp.zeros((1, half), F32)
                for b in range(blocks):
                    e = jnp.exp2(s_s[b * T : (b + 1) * T, lanes] - top)
                    s_s[b * T : (b + 1) * T, lanes] = e
                    row_total = row_total + jnp.sum(e, axis=0, keepdims=True)
                inverse = 1.0 / row_total
                for b in range(blocks):
                    probs[i, b * T : (b + 1) * T, lanes] = (s_s[b * T : (b + 1) * T, lanes] * inverse).astype(BF)

        by_window(ends, i, run)
        return 0

    lax.fori_loop(0, GROUPS, query_block, 0)


def gather_rows(blocks, vs, gs):
    me = lax.axis_index("ctx")
    for o, block in zip(ORDER, blocks):
        c = lax.rem(me - o + GROUPS, GROUPS)
        vs[pl.ds(pl.multiple_of(c * T, T), T), :] = block[:, 0:D]
        for j in range(GQ):
            gs[c, j * T : (j + 1) * T, :] = block[:, D * (1 + j) : D * (2 + j)]


def gradients(lengths_ref, kt, qs, probs, vs, gs, dk, dv, back, pg_s, db_s):
    eye = ones_where(iota((T, T), 0) == iota((T, T), 1)).astype(BF)
    factor = 1.0 / math.sqrt(D)
    ends = ends_of(lengths_ref)
    half = 2 * T

    def query_block(i, _):
        def run(blocks):
            start = pl.multiple_of((i - (blocks - 1)) * T, T)
            width = blocks * T
            window = pl.ds(start, width)
            for h in range(2):
                lanes = slice(h * half, (h + 1) * half)
                g = gs[i, lanes, :]
                delta = jnp.zeros((1, half), F32)
                for b in range(blocks):
                    rows = slice(b * T, (b + 1) * T)
                    pg = mm_nt(vs[pl.ds(start + b * T, T), :], g)
                    pg_s[rows, lanes] = pg
                    delta = delta + jnp.sum(probs[i, rows, lanes].astype(F32) * pg, axis=0, keepdims=True)
                for b in range(blocks):
                    rows = slice(b * T, (b + 1) * T)
                    db_s[rows, lanes] = (probs[i, rows, lanes].astype(F32) * (pg_s[rows, lanes] - delta)).astype(BF)
            dv[window, :] += mm(probs[i, 0:width, :], gs[i])
            dk[window, :] += mm(db_s[0:width, :], qs[i])
            dq_t = (mm(kt[:, window], db_s[0:width, :]) * factor).astype(BF)
            for j in range(GQ):
                dq = mm_nt(eye, dq_t[:, j * T : (j + 1) * T]).astype(BF)
                back[pl.ds(pl.multiple_of(i * T, T), T), j * D : (j + 1) * D] = dq

        by_window(ends, i, run)
        return 0

    lax.fori_loop(0, GROUPS, query_block, 0)


def grad_kernel(lengths_ref, kt, qs, probs, place_m, *refs):
    blocks, outs, packed = refs[:GROUPS], refs[GROUPS : 2 * GROUPS], refs[2 * GROUPS]
    dk, dv, vs, gs, back, pg_s, db_s = refs[2 * GROUPS + 1 :]
    me = lax.axis_index("ctx")
    gather_rows(blocks, vs, gs)
    dk[...] = jnp.zeros_like(dk)
    dv[...] = jnp.zeros_like(dv)
    gradients(lengths_ref, kt, qs, probs, vs, gs, dk, dv, back, pg_s, db_s)
    for o, out in zip(ORDER, outs):
        c = lax.rem(me + o, GROUPS)
        out[...] = back[pl.ds(pl.multiple_of(c * T, T), T), 0:BW]
    factor = 1.0 / math.sqrt(D)
    for pair in range(GROUPS // 2):
        rows = slice(pair * 2 * T, (pair + 1) * 2 * T)
        y = jnp.concatenate(
            [back[rows, BW : BW + D], (dk[rows, :] * factor).astype(BF), dv[rows, :].astype(BF)], axis=1
        )
        packed[:, 16 * pair : 16 * pair + 16, :] = mm(place_m[pair], y).astype(BF).reshape(S_DP, 16, BW)


def restore_b_kernel(r_ref, route_ref, *refs):
    outs, rows = refs[:GROUPS], refs[GROUPS]
    me = lax.axis_index("ctx")
    for pair in range(GROUPS // 2):
        r = r_ref[:, 16 * pair : 16 * pair + 16, :].reshape(2 * SLOTS, BW)
        for low in range(2):
            c = 2 * pair + low
            route_rows = jnp.broadcast_to(route_ref[8 * c : 8 * c + 1, :], (T, T))
            _, route_cols, sub_rank = rows_and_columns(route_rows)
            slot = (route_cols[:, 0:1] * (2 * CAP) + low * CAP + sub_rank).astype(jnp.int32)
            pick = ones_where(iota((T, 2 * SLOTS), 1) == slot).astype(BF)
            rows[c * T : (c + 1) * T, :] = mm(pick, r).astype(BF)
    for o, out in zip(ORDER, outs):
        c = lax.rem(me + o, GROUPS)
        out[...] = rows[pl.ds(pl.multiple_of(c * T, T), T), :]


def pack_back_kernel(m_ref, *refs):
    blocks, out = refs[:GROUPS], refs[GROUPS + 1]
    me = lax.axis_index("ctx")
    for o, block in zip(ORDER, blocks):
        g = lax.rem(me - o + GROUPS, GROUPS)
        out[:, pl.ds(pl.multiple_of(g * BW, D), BW)] = mm(m_ref[...], block[...]).astype(BF)


def finish_kernel(routes_ref, r_ref, *refs):
    blocks, (dq, dk, dv) = refs[:GROUPS], refs[GROUPS:]
    me = lax.axis_index("ctx")
    route_rows = jnp.broadcast_to(routes_ref[...].astype(F32), (T, T))
    _, route_cols, sub_rank = rows_and_columns(route_rows)
    slot = (route_cols[:, 0:1] * CAP + sub_rank).astype(jnp.int32)
    pick = ones_where(iota((T, SLOTS), 1) == slot).astype(BF)
    for g in range(GROUPS):
        dq[:, g * GQ * D : g * GQ * D + BW] = mm(pick, r_ref[:, g * BW : (g + 1) * BW]).astype(BF)
    for o, block in zip(ORDER, blocks):
        g = lax.rem(me - o + GROUPS, GROUPS)
        dq[:, pl.ds(pl.multiple_of(g * GQ * D + BW, D), D)] = block[:, 0:D]
        dk[:, pl.ds(pl.multiple_of(g * D, D), D)] = block[:, D : 2 * D]
        dv[:, pl.ds(pl.multiple_of(g * D, D), D)] = block[:, 2 * D : 3 * D]


def call(kernel, shapes, args, scratch=(), smem=0, hbm=(), vmem=32, flops=0):
    size = sum(math.prod(s.shape) * s.dtype.itemsize for s in (*shapes, *args))
    specs = [
        pl.BlockSpec(memory_space=pltpu.SMEM if i < smem else pltpu.HBM if i in hbm else pltpu.VMEM)
        for i in range(len(args) + len(shapes))
    ]
    return pl.pallas_call(
        kernel,
        out_shape=list(shapes),
        in_specs=specs[: len(args)],
        out_specs=specs[len(args) :],
        scratch_shapes=list(scratch),
        name=kernel.__name__,
        compiler_params=pltpu.CompilerParams(vmem_limit_bytes=vmem * 1024 * 1024),
        cost_estimate=pl.CostEstimate(flops=flops, bytes_accessed=size, transcendentals=0),
    )(*args)


def shape(*dims, dtype=BF):
    return jax.ShapeDtypeStruct(dims, dtype)


def swap(blocks):
    n = len(blocks)
    return [
        block if o == 0 else lax.ppermute(block, "ctx", [(i, (i + o) % n) for i in range(n)])
        for o, block in zip(ORDER, blocks)
    ]


def exchange(packed):
    return lax.all_to_all(packed, "dp", split_axis=0, concat_axis=0, tiled=True)


def body(queries, key_heads, value_heads, out_grad, routes, doc_lengths):
    q, k, v, g = queries[0], key_heads[0], value_heads[0], out_grad[0]
    *b_blocks, a_packed = call(
        enter_kernel,
        [shape((1 + GQ) * T + 16, D)] * GROUPS + [shape(SLOTS, GROUPS * FW)],
        [routes, k, q, v, g],
        [
            pltpu.VMEM((T, GROUPS * D), BF),
            pltpu.VMEM((T, GROUPS * GQ * D), BF),
            pltpu.VMEM((T, GROUPS * D), BF),
            pltpu.VMEM((T, GROUPS * GQ * D), BF),
            pltpu.VMEM((SLOTS, GROUPS * FW), BF),
            pltpu.VMEM((16, T), BF),
            pltpu.SemaphoreType.DMA((2, GROUPS // 2 + 1)),
            pltpu.SemaphoreType.DMA((GROUPS // 2,)),
            pltpu.SemaphoreType.DMA((GROUPS, 2 + GQ)),
        ],
        hbm=range(1, 6 + GROUPS),
        vmem=60,
        flops=2 * SLOTS * T * GROUPS * FW,
    )
    b_arrived = swap(b_blocks)
    a_arrived = exchange(a_packed.reshape(S_DP, CAP, GROUPS * FW)).reshape(SLOTS, GROUPS * FW)
    place, *a_blocks = call(
        unpack_a_kernel,
        [shape(SLOTS, T)] + [shape(T, FW)] * GROUPS,
        [a_arrived],
        flops=2 * SLOTS * T * GROUPS * FW,
    )
    a_blocks = swap(a_blocks)
    b_packed, every_route = call(
        pack_b_kernel,
        [shape(S_DP, GROUPS * CAP, FW), shape(GROUPS * 8, T, dtype=F32)],
        [*b_arrived, place],
        [
            pltpu.VMEM((SEQ, FW), BF),
            pltpu.VMEM((S_DP, GROUPS * CAP, FW), BF),
            pltpu.SemaphoreType.DMA((GROUPS // 2,)),
        ],
        hbm=(GROUPS, GROUPS + 1),
        flops=2 * 2 * SLOTS * SEQ * FW,
    )
    b_seq = exchange(b_packed)
    place_b, ks, kt, qs, probs = call(
        scores_kernel,
        [
            shape(GROUPS // 2, 2 * SLOTS, 2 * T),
            shape(SEQ, D),
            shape(D, SEQ),
            shape(GROUPS, GQ * T, D),
            shape(GROUPS, WINDOW * T, GQ * T),
        ],
        [doc_lengths, b_seq],
        [pltpu.VMEM((WINDOW * T, GQ * T), F32)],
        smem=1,
        flops=2 * 2 * SLOTS * SEQ * FW + 2 * 24 * T * T * GQ * D,
    )

    *dq_blocks, back_packed = call(
        grad_kernel,
        [shape(T, BW)] * GROUPS + [shape(S_DP, GROUPS * CAP, BW)],
        [doc_lengths, kt, qs, probs, place_b, *a_blocks],
        [
            pltpu.VMEM((SEQ, D), F32),
            pltpu.VMEM((SEQ, D), F32),
            pltpu.VMEM((SEQ, D), BF),
            pltpu.VMEM((GROUPS, GQ * T, D), BF),
            pltpu.VMEM((SEQ, GQ * D), BF),
            pltpu.VMEM((WINDOW * T, GQ * T), F32),
            pltpu.VMEM((WINDOW * T, GQ * T), BF),
        ],
        smem=1,
        flops=4 * 2 * 24 * T * T * GQ * D,
    )
    dq_arrived = swap(dq_blocks)
    back_arrived = exchange(back_packed)
    rest_blocks = call(
        restore_b_kernel,
        [shape(T, BW)] * GROUPS,
        [back_arrived, every_route],
        [pltpu.VMEM((SEQ, BW), BF)],
        flops=2 * 2 * SLOTS * SEQ * BW,
    )
    rest_arrived = swap(rest_blocks)
    (dq_packed,) = call(
        pack_back_kernel,
        [shape(SLOTS, GROUPS * BW)],
        [place, *dq_arrived, rest_blocks[0]],
        hbm=(1 + GROUPS,),
        flops=2 * SLOTS * T * GROUPS * BW,
    )
    dq_back = exchange(dq_packed.reshape(S_DP, CAP, GROUPS * BW)).reshape(SLOTS, GROUPS * BW)
    dq, dk, dv = call(
        finish_kernel,
        [shape(T, GROUPS * GQ * D), shape(T, GROUPS * D), shape(T, GROUPS * D)],
        [routes, dq_back, *rest_arrived],
        flops=2 * SLOTS * T * GROUPS * BW,
    )
    return dq[None], dk[None], dv[None]


def solution(mesh):
    return jax.shard_map(
        body,
        mesh=mesh,
        in_specs=(
            P("dp", "ctx", None),
            P("dp", "ctx", None),
            P("dp", "ctx", None),
            P("dp", "ctx", None),
            P("dp", "ctx"),
            P("dp", None),
        ),
        out_specs=(P("dp", "ctx", None), P("dp", "ctx", None), P("dp", "ctx", None)),
        check_vma=False,
    )
```

```python
import functools
import math

import jax
import jax.numpy as jnp
from jax import lax
from jax.experimental import pallas as pl
from jax.experimental.pallas import tpu as pltpu
from jax.sharding import PartitionSpec as P

GROUPS = 8
GQ = 4
D = 128
T = 128
NDOC = 8
CAP = 8
S_DP = 32
SLOTS = S_DP * CAP
SEQ = GROUPS * T
FW = (1 + GQ) * D
BW = 3 * D
MARK = 1e30
BF = jnp.bfloat16
F32 = jnp.float32
NEG = -1e30
ORDER = (0, 4, 3, 5, 2, 6, 1, 7)
WINDOW = 5


def mm(a, b):
    return jnp.dot(a, b, preferred_element_type=F32)


def mm_nt(a, b):
    return lax.dot_general(a, b, (((1,), (1,)), ((), ())), preferred_element_type=F32)


def iota(shape, dim):
    return lax.broadcasted_iota(jnp.int32, shape, dim)


def ones_where(cond):
    return jnp.where(cond, 1.0, 0.0).astype(F32)


def rows_and_columns(route_rows):
    eye = ones_where(iota((T, T), 0) == iota((T, T), 1)).astype(BF)
    route_cols = mm_nt(eye, route_rows.astype(BF))
    same = route_rows == route_cols
    lane_rank = jnp.sum(ones_where(same & (iota((T, T), 0) < iota((T, T), 1))), axis=0, keepdims=True)
    sub_rank = jnp.sum(ones_where(same & (iota((T, T), 1) < iota((T, T), 0))), axis=1, keepdims=True)
    return lane_rank, route_cols, sub_rank


def enter_kernel(routes_ref, k_hbm, q_hbm, v_hbm, g_hbm, *refs):
    outs, packed_hbm = refs[:GROUPS], refs[GROUPS]
    k_ref, q_ref, v_ref, g_ref, packed, route_tile, in_sem, out_sem, stack_sem = refs[GROUPS + 1 :]
    me = lax.axis_index("ctx")
    step = 2
    arriving, leaving = [], []
    stacking = (
        pltpu.make_async_copy(q_hbm, q_ref, in_sem.at[0, GROUPS // step]),
        pltpu.make_async_copy(k_hbm, k_ref, in_sem.at[1, GROUPS // step]),
    )
    for copy in stacking:
        copy.start()
    for n, g in enumerate(range(0, GROUPS, step)):
        vs, gs = slice(g * D, (g + step) * D), slice(g * GQ * D, (g + step) * GQ * D)
        pair = (
            pltpu.make_async_copy(v_hbm.at[:, vs], v_ref.at[:, vs], in_sem.at[0, n]),
            pltpu.make_async_copy(g_hbm.at[:, gs], g_ref.at[:, gs], in_sem.at[1, n]),
        )
        arriving.append(pair)
        for copy in pair:
            copy.start()
    route_tile[...] = jnp.broadcast_to(routes_ref[...].astype(F32), (16, T)).astype(BF)
    for copy in stacking:
        copy.wait()
    for n, (o, out) in enumerate(zip(ORDER, outs)):
        to = lax.rem(me + o, GROUPS)
        parts = [(k_ref.at[:, pl.ds(pl.multiple_of(to * D, D), D)], out.at[0:T, :])]
        for j in range(GQ):
            lanes = pl.ds(pl.multiple_of(to * GQ * D + j * D, D), D)
            parts.append((q_ref.at[:, lanes], out.at[(1 + j) * T : (2 + j) * T, :]))
        parts.append((route_tile, out.at[(1 + GQ) * T : (1 + GQ) * T + 16, :]))
        for m, (source, target) in enumerate(parts):
            leaving.append(pltpu.make_async_copy(source, target, stack_sem.at[n, m]))
            leaving[-1].start()
    route_rows = jnp.broadcast_to(routes_ref[...].astype(F32), (T, T))
    lane_rank, _, _ = rows_and_columns(route_rows)
    slot = (route_rows[0:1, :] * CAP + lane_rank).astype(jnp.int32)
    onehot = ones_where(iota((SLOTS, T), 0) == slot).astype(BF)
    unused = 1.0 - mm(onehot, jnp.ones((T, D), BF))
    for n, pair in enumerate(arriving):
        for copy in pair:
            copy.wait()
        for g in range(n * step, (n + 1) * step):
            values = mm(onehot, v_ref[:, g * D : (g + 1) * D])
            if g == 0:
                values = values + unused * MARK
            packed[:, g * FW : g * FW + D] = values.astype(BF)
            packed[:, g * FW + D : (g + 1) * FW] = mm(onehot, g_ref[:, g * GQ * D : (g + 1) * GQ * D]).astype(BF)
        lanes = slice(n * step * FW, (n + 1) * step * FW)
        leaving.append(pltpu.make_async_copy(packed.at[:, lanes], packed_hbm.at[:, lanes], out_sem.at[n]))
        leaving[-1].start()
    for copy in leaving:
        copy.wait()


def unpack_a_kernel(r_ref, m_ref, done, *outs):
    done[...] = jnp.zeros_like(done)
    me = lax.axis_index("ctx")
    flags = ones_where(r_ref[:, 0:D].astype(F32) < 0.5 * MARK)
    lower = ones_where(iota((SLOTS, SLOTS), 1) < iota((SLOTS, SLOTS), 0)).astype(BF)
    flags_b = flags.astype(BF)
    place = mm(lower, flags_b)
    hit = (place == iota((SLOTS, T), 1).astype(F32)) & (flags > 0.5)
    m_ref[...] = ones_where(hit).astype(BF)
    first = ones_where(iota((T, D), 1) == 0).astype(BF)
    flags_t = mm_nt(first, flags_b)
    place_t = mm_nt(flags_t.astype(BF), lower)
    hit_t = (place_t == iota((T, SLOTS), 0).astype(F32)) & (flags_t > 0.5)
    pick = ones_where(hit_t).astype(BF)
    for o, out in zip(ORDER, outs):
        to = lax.rem(me + o, GROUPS)
        out[...] = mm(pick, r_ref[:, pl.ds(pl.multiple_of(to * FW, D), FW)]).astype(BF)


def source_of(me, position):
    return lax.rem(me - ORDER[position] + GROUPS, GROUPS)


HALF = GROUPS // 2


def pack_b_kernel(first_pair, *refs):
    blocks, (out_hbm, route_out, rows, out, out_sem) = refs[:HALF], refs[HALF + 2 :]
    sent = []
    for n in range(HALF // 2):
        pair = first_pair + n
        slots = []
        for low in range(2):
            position = 2 * n + low
            block = blocks[position]
            for j in range(1 + GQ):
                rows[position * T : (position + 1) * T, j * D : (j + 1) * D] = block[j * T : (j + 1) * T, :]
            route_out[8 * position : 8 * position + 8, :] = block[(1 + GQ) * T :, :].astype(F32)[0:8, :]
            route_rows = jnp.broadcast_to(route_out[8 * position : 8 * position + 1, :], (T, T))
            lane_rank, _, _ = rows_and_columns(route_rows)
            slots.append(route_rows[0:1, :] * (2 * CAP) + low * CAP + lane_rank)
        slot = jnp.concatenate(slots, axis=1).astype(jnp.int32)
        onehot = ones_where(iota((2 * SLOTS, 2 * T), 0) == slot).astype(BF)
        unused = 1.0 - mm(onehot, jnp.ones((2 * T, D), BF))
        x = mm(onehot, rows[2 * T * n : 2 * T * (n + 1), :])
        lines = slice(16 * n, 16 * n + 16)
        out[:, lines, 0:D] = (x[:, 0:D] + unused * MARK).astype(BF).reshape(S_DP, 16, D)
        out[:, lines, D:FW] = x[:, D:FW].astype(BF).reshape(S_DP, 16, FW - D)
        sent.append(
            pltpu.make_async_copy(
                out.at[:, lines, :], out_hbm.at[:, 16 * pair : 16 * pair + 16, :], out_sem.at[n]
            )
        )
        sent[-1].start()
    for copy in sent:
        copy.wait()


def ends_of(lengths_ref):
    ends = []
    total = jnp.int32(0)
    for d in range(NDOC):
        total = total + lengths_ref[0, d]
        ends.append(total)
    return ends


def by_window(ends, i, run):
    first_start = jnp.int32(0)
    for end in ends:
        first_start = jnp.where(i * T >= end, end, first_start)
    reach = i - first_start // T + 1
    for blocks in range(1, WINDOW + 1):
        pl.when(reach == blocks)(functools.partial(run, blocks))


def scores_kernel(lengths_ref, r_ref, place_m, ks, kt, qs, probs, s_s):
    eye = ones_where(iota((T, T), 0) == iota((T, T), 1)).astype(BF)
    two = 2 * SLOTS
    row, col = iota((two, two), 0), iota((two, two), 1)
    lower = ones_where((col < row) & (((row ^ col) & CAP) == 0)).astype(BF)
    slot_low = iota((two, T), 0) & CAP
    first = ones_where(iota((8, D), 1) == 0).astype(BF)
    token = iota((2 * T, two), 0)
    mine = (iota((2 * T, two), 1) & CAP) == (token >> 7) * CAP
    token = (token & (T - 1)).astype(F32)
    me = lax.axis_index("ctx")
    for pair in range(GROUPS // 2):
        r = r_ref[:, 16 * pair : 16 * pair + 16, :].reshape(two, FW)
        flags = ones_where(r[:, 0:D].astype(F32) < 0.5 * MARK)
        flags_b = flags.astype(BF)
        place = mm(lower, flags_b)
        hit = (place == iota((two, T), 1).astype(F32)) & (flags > 0.5)
        for low in range(2):
            place_m[pair, :, low * T : (low + 1) * T] = ones_where(hit & (slot_low == low * CAP)).astype(BF)
        flags_t = mm_nt(first, flags_b)
        place_t = mm_nt(flags_t.astype(BF), lower)
        place_t = jnp.where(flags_t > 0.5, place_t, -1.0)[0:1, :]
        pick = ones_where((place_t == token) & mine).astype(BF)
        x = mm(pick, r).astype(BF)
        for low in range(2):
            c = source_of(me, 2 * pair + low)
            rows = pl.ds(pl.multiple_of(c * T, T), T)
            part = x[low * T : (low + 1) * T, :]
            ks[rows, :] = part[:, 0:D]
            kt[:, rows] = mm_nt(eye, part[:, 0:D]).astype(BF)
            for j in range(GQ):
                qs[c, j * T : (j + 1) * T, :] = part[:, D * (1 + j) : D * (2 + j)]
    ends = ends_of(lengths_ref)
    half = 2 * T
    scale = math.log2(math.e) / math.sqrt(D)

    def query_block(i, _):
        q_pos = i * T + lax.rem(iota((1, half), 1), T)
        doc_start = jnp.zeros((1, half), jnp.int32)
        for end in ends:
            doc_start = jnp.where(q_pos >= end, end, doc_start)

        def run(blocks):
            start = pl.multiple_of((i - (blocks - 1)) * T, T)
            for h in range(2):
                lanes = slice(h * half, (h + 1) * half)
                q = qs[i, lanes, :]
                top = None
                for b in range(blocks):
                    s = mm_nt(ks[pl.ds(start + b * T, T), :], q) * scale
                    k_pos = start + b * T + iota((T, half), 0)
                    keep = k_pos >= doc_start
                    if b == blocks - 1:
                        keep = keep & (k_pos <= q_pos)
                    s = jnp.where(keep, s, NEG)
                    s_s[b * T : (b + 1) * T, lanes] = s
                    high = jnp.max(s, axis=0, keepdims=True)
                    top = high if top is None else jnp.maximum(top, high)
                row_total = jnp.zeros((1, half), F32)
                for b in range(blocks):
                    e = jnp.exp2(s_s[b * T : (b + 1) * T, lanes] - top)
                    s_s[b * T : (b + 1) * T, lanes] = e
                    row_total = row_total + jnp.sum(e, axis=0, keepdims=True)
                inverse = 1.0 / row_total
                for b in range(blocks):
                    probs[i, b * T : (b + 1) * T, lanes] = (s_s[b * T : (b + 1) * T, lanes] * inverse).astype(BF)

        by_window(ends, i, run)
        return 0

    lax.fori_loop(0, GROUPS, query_block, 0)


def gather_rows(blocks, vs, gs):
    me = lax.axis_index("ctx")
    for o, block in zip(ORDER, blocks):
        c = lax.rem(me - o + GROUPS, GROUPS)
        vs[pl.ds(pl.multiple_of(c * T, T), T), :] = block[:, 0:D]
        for j in range(GQ):
            gs[c, j * T : (j + 1) * T, :] = block[:, D * (1 + j) : D * (2 + j)]


def gradients(lengths_ref, kt, qs, probs, vs, gs, dk, dv, back, pg_s, db_s):
    eye = ones_where(iota((T, T), 0) == iota((T, T), 1)).astype(BF)
    factor = 1.0 / math.sqrt(D)
    ends = ends_of(lengths_ref)
    half = 2 * T

    def query_block(i, _):
        def run(blocks):
            start = pl.multiple_of((i - (blocks - 1)) * T, T)
            width = blocks * T
            window = pl.ds(start, width)
            for h in range(2):
                lanes = slice(h * half, (h + 1) * half)
                g = gs[i, lanes, :]
                delta = jnp.zeros((1, half), F32)
                for b in range(blocks):
                    rows = slice(b * T, (b + 1) * T)
                    pg = mm_nt(vs[pl.ds(start + b * T, T), :], g)
                    pg_s[rows, lanes] = pg
                    delta = delta + jnp.sum(probs[i, rows, lanes].astype(F32) * pg, axis=0, keepdims=True)
                for b in range(blocks):
                    rows = slice(b * T, (b + 1) * T)
                    db_s[rows, lanes] = (probs[i, rows, lanes].astype(F32) * (pg_s[rows, lanes] - delta)).astype(BF)
            dv[window, :] += mm(probs[i, 0:width, :], gs[i])
            dk[window, :] += mm(db_s[0:width, :], qs[i])
            dq_t = (mm(kt[:, window], db_s[0:width, :]) * factor).astype(BF)
            for j in range(GQ):
                dq = mm_nt(eye, dq_t[:, j * T : (j + 1) * T]).astype(BF)
                back[pl.ds(pl.multiple_of(i * T, T), T), j * D : (j + 1) * D] = dq

        by_window(ends, i, run)
        return 0

    lax.fori_loop(0, GROUPS, query_block, 0)


def grad_kernel(lengths_ref, kt, qs, probs, place_m, *refs):
    blocks, outs, packed = refs[:GROUPS], refs[GROUPS : 2 * GROUPS], refs[2 * GROUPS]
    dk, dv, vs, gs, back, pg_s, db_s = refs[2 * GROUPS + 1 :]
    me = lax.axis_index("ctx")
    gather_rows(blocks, vs, gs)
    dk[...] = jnp.zeros_like(dk)
    dv[...] = jnp.zeros_like(dv)
    gradients(lengths_ref, kt, qs, probs, vs, gs, dk, dv, back, pg_s, db_s)
    for o, out in zip(ORDER, outs):
        c = lax.rem(me + o, GROUPS)
        out[...] = back[pl.ds(pl.multiple_of(c * T, T), T), 0:BW]
    factor = 1.0 / math.sqrt(D)
    for pair in range(GROUPS // 2):
        parts = []
        for low in range(2):
            rows = pl.ds(pl.multiple_of(source_of(me, 2 * pair + low) * T, T), T)
            parts.append(
                jnp.concatenate(
                    [back[rows, BW : BW + D], (dk[rows, :] * factor).astype(BF), dv[rows, :].astype(BF)], axis=1
                )
            )
        y = jnp.concatenate(parts, axis=0)
        packed[:, 16 * pair : 16 * pair + 16, :] = mm(place_m[pair], y).astype(BF).reshape(S_DP, 16, BW)


def restore_b_kernel(r_ref, early_ref, late_ref, *refs):
    outs, (done, rows) = refs[:GROUPS], refs[GROUPS:]
    done[...] = jnp.zeros_like(done)
    me = lax.axis_index("ctx")
    for pair in range(GROUPS // 2):
        r = r_ref[:, 16 * pair : 16 * pair + 16, :].reshape(2 * SLOTS, BW)
        for low in range(2):
            route_ref, line = (early_ref, late_ref)[pair // 2], 8 * (2 * (pair % 2) + low)
            route_rows = jnp.broadcast_to(route_ref[line : line + 1, :], (T, T))
            _, route_cols, sub_rank = rows_and_columns(route_rows)
            slot = (route_cols[:, 0:1] * (2 * CAP) + low * CAP + sub_rank).astype(jnp.int32)
            pick = ones_where(iota((T, 2 * SLOTS), 1) == slot).astype(BF)
            c = source_of(me, 2 * pair + low)
            rows[pl.ds(pl.multiple_of(c * T, T), T), :] = mm(pick, r).astype(BF)
    for o, out in zip(ORDER, outs):
        c = lax.rem(me + o, GROUPS)
        out[...] = rows[pl.ds(pl.multiple_of(c * T, T), T), :]


def pack_back_kernel(m_ref, *refs):
    blocks, out = refs[:GROUPS], refs[GROUPS + 1]
    me = lax.axis_index("ctx")
    for o, block in zip(ORDER, blocks):
        g = lax.rem(me - o + GROUPS, GROUPS)
        out[:, pl.ds(pl.multiple_of(g * BW, D), BW)] = mm(m_ref[...], block[...]).astype(BF)


def finish_kernel(routes_ref, r_ref, *refs):
    blocks, (dq, dk, dv) = refs[:GROUPS], refs[GROUPS:]
    me = lax.axis_index("ctx")
    route_rows = jnp.broadcast_to(routes_ref[...].astype(F32), (T, T))
    _, route_cols, sub_rank = rows_and_columns(route_rows)
    slot = (route_cols[:, 0:1] * CAP + sub_rank).astype(jnp.int32)
    pick = ones_where(iota((T, SLOTS), 1) == slot).astype(BF)
    for g in range(GROUPS):
        dq[:, g * GQ * D : g * GQ * D + BW] = mm(pick, r_ref[:, g * BW : (g + 1) * BW]).astype(BF)
    for o, block in zip(ORDER, blocks):
        g = lax.rem(me - o + GROUPS, GROUPS)
        dq[:, pl.ds(pl.multiple_of(g * GQ * D + BW, D), D)] = block[:, 0:D]
        dk[:, pl.ds(pl.multiple_of(g * D, D), D)] = block[:, D : 2 * D]
        dv[:, pl.ds(pl.multiple_of(g * D, D), D)] = block[:, 2 * D : 3 * D]


def call(kernel, shapes, args, scratch=(), smem=0, hbm=(), vmem=32, flops=0, aliases=None):
    size = sum(math.prod(s.shape) * s.dtype.itemsize for s in (*shapes, *args))
    specs = [
        pl.BlockSpec(memory_space=pltpu.SMEM if i < smem else pltpu.HBM if i in hbm else pltpu.VMEM)
        for i in range(len(args) + len(shapes))
    ]
    return pl.pallas_call(
        kernel,
        out_shape=list(shapes),
        in_specs=specs[: len(args)],
        out_specs=specs[len(args) :],
        scratch_shapes=list(scratch),
        name=getattr(kernel, "func", kernel).__name__,
        input_output_aliases=aliases or {},
        compiler_params=pltpu.CompilerParams(vmem_limit_bytes=vmem * 1024 * 1024),
        cost_estimate=pl.CostEstimate(flops=flops, bytes_accessed=size, transcendentals=0),
    )(*args)


def shape(*dims, dtype=BF):
    return jax.ShapeDtypeStruct(dims, dtype)


def swap(blocks):
    n = len(blocks)
    return [
        block if o == 0 else lax.ppermute(block, "ctx", [(i, (i + o) % n) for i in range(n)])
        for o, block in zip(ORDER, blocks)
    ]


def exchange(packed):
    return lax.all_to_all(packed, "dp", split_axis=0, concat_axis=0, tiled=True)


def body(queries, key_heads, value_heads, out_grad, routes, doc_lengths):
    q, k, v, g = queries[0], key_heads[0], value_heads[0], out_grad[0]
    *b_blocks, a_packed = call(
        enter_kernel,
        [shape((1 + GQ) * T + 16, D)] * GROUPS + [shape(SLOTS, GROUPS * FW)],
        [routes, k, q, v, g],
        [
            pltpu.VMEM((T, GROUPS * D), BF),
            pltpu.VMEM((T, GROUPS * GQ * D), BF),
            pltpu.VMEM((T, GROUPS * D), BF),
            pltpu.VMEM((T, GROUPS * GQ * D), BF),
            pltpu.VMEM((SLOTS, GROUPS * FW), BF),
            pltpu.VMEM((16, T), BF),
            pltpu.SemaphoreType.DMA((2, GROUPS // 2 + 1)),
            pltpu.SemaphoreType.DMA((GROUPS // 2,)),
            pltpu.SemaphoreType.DMA((GROUPS, 2 + GQ)),
        ],
        hbm=range(1, 6 + GROUPS),
        vmem=60,
        flops=2 * SLOTS * T * GROUPS * FW,
    )
    b_arrived = swap(b_blocks)
    a_arrived = exchange(a_packed.reshape(S_DP, CAP, GROUPS * FW)).reshape(SLOTS, GROUPS * FW)
    place, unpacked, *a_blocks = call(
        unpack_a_kernel,
        [shape(SLOTS, T), shape(8, T, dtype=F32)] + [shape(T, FW)] * GROUPS,
        [a_arrived],
        flops=2 * SLOTS * T * GROUPS * FW,
    )
    a_blocks = swap(a_blocks)

    def pack_b(first_pair, blocks, other, after, aliases):
        return call(
            functools.partial(pack_b_kernel, first_pair),
            [shape(S_DP, GROUPS * CAP, FW), shape(HALF * 8, T, dtype=F32)],
            [*blocks, other, after],
            [
                pltpu.VMEM((HALF * T, FW), BF),
                pltpu.VMEM((S_DP, HALF * CAP, FW), BF),
                pltpu.SemaphoreType.DMA((HALF // 2,)),
            ],
            hbm=(HALF, HALF + 2) if aliases else (HALF + 2,),
            flops=2 * SLOTS * SEQ * FW,
            aliases=aliases,
        )

    b_packed, early_route = pack_b(0, b_arrived[:HALF], routes, routes, {})
    b_packed, late_route = pack_b(HALF // 2, b_arrived[HALF:], b_packed, unpacked, {HALF: 0})
    b_seq = exchange(b_packed)
    place_b, ks, kt, qs, probs = call(
        scores_kernel,
        [
            shape(GROUPS // 2, 2 * SLOTS, 2 * T),
            shape(SEQ, D),
            shape(D, SEQ),
            shape(GROUPS, GQ * T, D),
            shape(GROUPS, WINDOW * T, GQ * T),
        ],
        [doc_lengths, b_seq],
        [pltpu.VMEM((WINDOW * T, GQ * T), F32)],
        smem=1,
        flops=2 * 2 * SLOTS * SEQ * FW + 2 * 24 * T * T * GQ * D,
    )

    *dq_blocks, back_packed = call(
        grad_kernel,
        [shape(T, BW)] * GROUPS + [shape(S_DP, GROUPS * CAP, BW)],
        [doc_lengths, kt, qs, probs, place_b, *a_blocks],
        [
            pltpu.VMEM((SEQ, D), F32),
            pltpu.VMEM((SEQ, D), F32),
            pltpu.VMEM((SEQ, D), BF),
            pltpu.VMEM((GROUPS, GQ * T, D), BF),
            pltpu.VMEM((SEQ, GQ * D), BF),
            pltpu.VMEM((WINDOW * T, GQ * T), F32),
            pltpu.VMEM((WINDOW * T, GQ * T), BF),
        ],
        smem=1,
        flops=4 * 2 * 24 * T * T * GQ * D,
    )
    dq_arrived = swap(dq_blocks)
    back_arrived = exchange(back_packed)
    *rest_blocks, restored = call(
        restore_b_kernel,
        [shape(T, BW)] * GROUPS + [shape(8, T, dtype=F32)],
        [back_arrived, early_route, late_route],
        [pltpu.VMEM((SEQ, BW), BF)],
        flops=2 * 2 * SLOTS * SEQ * BW,
    )
    rest_arrived = swap(rest_blocks)
    (dq_packed,) = call(
        pack_back_kernel,
        [shape(SLOTS, GROUPS * BW)],
        [place, *dq_arrived, restored],
        flops=2 * SLOTS * T * GROUPS * BW,
    )
    dq_back = exchange(dq_packed.reshape(S_DP, CAP, GROUPS * BW)).reshape(SLOTS, GROUPS * BW)
    dq, dk, dv = call(
        finish_kernel,
        [shape(T, GROUPS * GQ * D), shape(T, GROUPS * D), shape(T, GROUPS * D)],
        [routes, dq_back, *rest_arrived],
        flops=2 * SLOTS * T * GROUPS * BW,
    )
    return dq[None], dk[None], dv[None]


def solution(mesh):
    return jax.shard_map(
        body,
        mesh=mesh,
        in_specs=(
            P("dp", "ctx", None),
            P("dp", "ctx", None),
            P("dp", "ctx", None),
            P("dp", "ctx", None),
            P("dp", "ctx"),
            P("dp", None),
        ),
        out_specs=(P("dp", "ctx", None), P("dp", "ctx", None), P("dp", "ctx", None)),
        check_vma=False,
    )
```

```python
import functools
import math

import jax
import jax.numpy as jnp
from jax import lax
from jax.experimental import pallas as pl
from jax.experimental.pallas import tpu as pltpu
from jax.sharding import PartitionSpec as P

GROUPS = 8
GQ = 4
D = 128
T = 128
NDOC = 8
CAP = 8
S_DP = 32
SLOTS = S_DP * CAP
SEQ = GROUPS * T
FW = (1 + GQ) * D
BW = 3 * D
MARK = 1e30
BF = jnp.bfloat16
F32 = jnp.float32
NEG = -1e30
ORDER = (0, 4, 3, 5, 2, 6, 1, 7)
WINDOW = 5


def mm(a, b):
    return jnp.dot(a, b, preferred_element_type=F32)


def mm_nt(a, b):
    return lax.dot_general(a, b, (((1,), (1,)), ((), ())), preferred_element_type=F32)


def iota(shape, dim):
    return lax.broadcasted_iota(jnp.int32, shape, dim)


def ones_where(cond):
    return jnp.where(cond, 1.0, 0.0).astype(F32)


def rows_and_columns(route_rows):
    eye = ones_where(iota((T, T), 0) == iota((T, T), 1)).astype(BF)
    route_cols = mm_nt(eye, route_rows.astype(BF))
    same = route_rows == route_cols
    lane_rank = jnp.sum(ones_where(same & (iota((T, T), 0) < iota((T, T), 1))), axis=0, keepdims=True)
    earlier = ones_where(same & (iota((T, T), 1) < iota((T, T), 0))).astype(BF)
    sub_rank = mm(earlier, jnp.ones((T, T), BF))
    return lane_rank, route_cols, sub_rank


def enter_kernel(routes_ref, k_hbm, q_hbm, v_hbm, g_hbm, *refs):
    outs, packed_hbm = refs[:GROUPS], refs[GROUPS]
    k_ref, q_ref, v_ref, g_ref, packed, route_tile, in_sem, out_sem, stack_sem = refs[GROUPS + 1 :]
    me = lax.axis_index("ctx")
    step = 2
    arriving, leaving = [], []
    for n, g in enumerate(range(0, GROUPS, step)):
        vs, gs = slice(g * D, (g + step) * D), slice(g * GQ * D, (g + step) * GQ * D)
        pair = (
            pltpu.make_async_copy(v_hbm.at[:, vs], v_ref.at[:, vs], in_sem.at[0, n]),
            pltpu.make_async_copy(g_hbm.at[:, gs], g_ref.at[:, gs], in_sem.at[1, n]),
        )
        arriving.append(pair)
        for copy in pair:
            copy.start()
    stacking = (
        pltpu.make_async_copy(q_hbm, q_ref, in_sem.at[0, GROUPS // step]),
        pltpu.make_async_copy(k_hbm, k_ref, in_sem.at[1, GROUPS // step]),
    )
    for copy in stacking:
        copy.start()
    route_tile[...] = jnp.broadcast_to(routes_ref[...].astype(F32), (16, T)).astype(BF)
    route_rows = jnp.broadcast_to(routes_ref[...].astype(F32), (T, T))
    lane_rank, _, _ = rows_and_columns(route_rows)
    slot = (route_rows[0:1, :] * CAP + lane_rank).astype(jnp.int32)
    onehot = ones_where(iota((SLOTS, T), 0) == slot).astype(BF)
    unused = 1.0 - mm(onehot, jnp.ones((T, D), BF))
    for n, pair in enumerate(arriving):
        for copy in pair:
            copy.wait()
        for g in range(n * step, (n + 1) * step):
            values = mm(onehot, v_ref[:, g * D : (g + 1) * D])
            if g == 0:
                values = values + unused * MARK
            packed[:, g * FW : g * FW + D] = values.astype(BF)
            packed[:, g * FW + D : (g + 1) * FW] = mm(onehot, g_ref[:, g * GQ * D : (g + 1) * GQ * D]).astype(BF)
        lanes = slice(n * step * FW, (n + 1) * step * FW)
        leaving.append(pltpu.make_async_copy(packed.at[:, lanes], packed_hbm.at[:, lanes], out_sem.at[n]))
        leaving[-1].start()
        if n == 0:
            for copy in stacking:
                copy.wait()
        for i in range(n * step, (n + 1) * step):
            to = lax.rem(me + ORDER[i], GROUPS)
            parts = [(k_ref.at[:, pl.ds(pl.multiple_of(to * D, D), D)], outs[i].at[0:T, :])]
            for j in range(GQ):
                lanes = pl.ds(pl.multiple_of(to * GQ * D + j * D, D), D)
                parts.append((q_ref.at[:, lanes], outs[i].at[(1 + j) * T : (2 + j) * T, :]))
            parts.append((route_tile, outs[i].at[(1 + GQ) * T : (1 + GQ) * T + 16, :]))
            for m, (source, target) in enumerate(parts):
                leaving.append(pltpu.make_async_copy(source, target, stack_sem.at[i, m]))
                leaving[-1].start()
    for copy in leaving:
        copy.wait()


def unpack_a_kernel(r_ref, m_ref, done, *outs):
    done[...] = jnp.zeros_like(done)
    me = lax.axis_index("ctx")
    flags = ones_where(r_ref[:, 0:D].astype(F32) < 0.5 * MARK)
    lower = ones_where(iota((SLOTS, SLOTS), 1) < iota((SLOTS, SLOTS), 0)).astype(BF)
    flags_b = flags.astype(BF)
    place = mm(lower, flags_b)
    hit = (place == iota((SLOTS, T), 1).astype(F32)) & (flags > 0.5)
    m_ref[...] = ones_where(hit).astype(BF)
    first = ones_where(iota((T, D), 1) == 0).astype(BF)
    flags_t = mm_nt(first, flags_b)
    place_t = mm_nt(flags_t.astype(BF), lower)
    hit_t = (place_t == iota((T, SLOTS), 0).astype(F32)) & (flags_t > 0.5)
    pick = ones_where(hit_t).astype(BF)
    for o, out in zip(ORDER, outs):
        to = lax.rem(me + o, GROUPS)
        out[...] = mm(pick, r_ref[:, pl.ds(pl.multiple_of(to * FW, D), FW)]).astype(BF)


def source_of(me, position):
    return lax.rem(me - ORDER[position] + GROUPS, GROUPS)


HALF = GROUPS // 2


def pack_b_kernel(first_pair, *refs):
    blocks, (out_hbm, route_out, rows, out, out_sem) = refs[:HALF], refs[HALF + 2 :]
    sent = []
    for n in range(HALF // 2):
        pair = first_pair + n
        slots = []
        for low in range(2):
            position = 2 * n + low
            block = blocks[position]
            for j in range(1 + GQ):
                rows[position * T : (position + 1) * T, j * D : (j + 1) * D] = block[j * T : (j + 1) * T, :]
            route_out[8 * position : 8 * position + 8, :] = block[(1 + GQ) * T :, :].astype(F32)[0:8, :]
            route_rows = jnp.broadcast_to(route_out[8 * position : 8 * position + 1, :], (T, T))
            lane_rank, _, _ = rows_and_columns(route_rows)
            slots.append(route_rows[0:1, :] * (2 * CAP) + low * CAP + lane_rank)
        slot = jnp.concatenate(slots, axis=1).astype(jnp.int32)
        onehot = ones_where(iota((2 * SLOTS, 2 * T), 0) == slot).astype(BF)
        unused = 1.0 - mm(onehot, jnp.ones((2 * T, D), BF))
        x = mm(onehot, rows[2 * T * n : 2 * T * (n + 1), :])
        lines = slice(16 * n, 16 * n + 16)
        out[:, lines, 0:D] = (x[:, 0:D] + unused * MARK).astype(BF).reshape(S_DP, 16, D)
        out[:, lines, D:FW] = x[:, D:FW].astype(BF).reshape(S_DP, 16, FW - D)
        sent.append(
            pltpu.make_async_copy(
                out.at[:, lines, :], out_hbm.at[:, 16 * pair : 16 * pair + 16, :], out_sem.at[n]
            )
        )
        sent[-1].start()
    for copy in sent:
        copy.wait()


def ends_of(lengths_ref):
    ends = []
    total = jnp.int32(0)
    for d in range(NDOC):
        total = total + lengths_ref[0, d]
        ends.append(total)
    return ends


def by_window(ends, i, run):
    first_start = jnp.int32(0)
    for end in ends:
        first_start = jnp.where(i * T >= end, end, first_start)
    reach = i - first_start // T + 1
    for blocks in range(1, WINDOW + 1):
        pl.when(reach == blocks)(functools.partial(run, blocks))


def scores_kernel(lengths_ref, r_ref, place_m, ks, qs, probs, s_s):
    two = 2 * SLOTS
    row, col = iota((two, two), 0), iota((two, two), 1)
    lower = ones_where((col < row) & (((row ^ col) & CAP) == 0)).astype(BF)
    slot_low = iota((two, T), 0) & CAP
    first = ones_where(iota((8, D), 1) == 0).astype(BF)
    token = iota((2 * T, two), 0)
    mine = (iota((2 * T, two), 1) & CAP) == (token >> 7) * CAP
    token = (token & (T - 1)).astype(F32)
    me = lax.axis_index("ctx")
    for pair in range(GROUPS // 2):
        r = r_ref[:, 16 * pair : 16 * pair + 16, :].reshape(two, FW)
        flags = ones_where(r[:, 0:D].astype(F32) < 0.5 * MARK)
        flags_b = flags.astype(BF)
        place = mm(lower, flags_b)
        hit = (place == iota((two, T), 1).astype(F32)) & (flags > 0.5)
        for low in range(2):
            place_m[pair, :, low * T : (low + 1) * T] = ones_where(hit & (slot_low == low * CAP)).astype(BF)
        flags_t = mm_nt(first, flags_b)
        place_t = mm_nt(flags_t.astype(BF), lower)
        place_t = jnp.where(flags_t > 0.5, place_t, -1.0)[0:1, :]
        pick = ones_where((place_t == token) & mine).astype(BF)
        x = mm(pick, r).astype(BF)
        for low in range(2):
            c = source_of(me, 2 * pair + low)
            rows = pl.ds(pl.multiple_of(c * T, T), T)
            part = x[low * T : (low + 1) * T, :]
            ks[rows, :] = part[:, 0:D]
            for j in range(GQ):
                qs[c, j * T : (j + 1) * T, :] = part[:, D * (1 + j) : D * (2 + j)]
    ends = ends_of(lengths_ref)
    half = 2 * T
    scale = math.log2(math.e) / math.sqrt(D)

    def query_block(i, _):
        q_pos = i * T + lax.rem(iota((1, half), 1), T)
        doc_start = jnp.zeros((1, half), jnp.int32)
        for end in ends:
            doc_start = jnp.where(q_pos >= end, end, doc_start)

        def run(blocks):
            start = pl.multiple_of((i - (blocks - 1)) * T, T)
            for h in range(2):
                lanes = slice(h * half, (h + 1) * half)
                q = qs[i, lanes, :]
                top = None
                for b in range(blocks):
                    s = mm_nt(ks[pl.ds(start + b * T, T), :], q) * scale
                    k_pos = start + b * T + iota((T, half), 0)
                    keep = k_pos >= doc_start
                    if b == blocks - 1:
                        keep = keep & (k_pos <= q_pos)
                    s = jnp.where(keep, s, NEG)
                    s_s[b * T : (b + 1) * T, lanes] = s
                    high = jnp.max(s, axis=0, keepdims=True)
                    top = high if top is None else jnp.maximum(top, high)
                row_total = jnp.zeros((1, half), F32)
                for b in range(blocks):
                    e = jnp.exp2(s_s[b * T : (b + 1) * T, lanes] - top)
                    s_s[b * T : (b + 1) * T, lanes] = e
                    row_total = row_total + jnp.sum(e, axis=0, keepdims=True)
                inverse = 1.0 / row_total
                for b in range(blocks):
                    probs[i, b * T : (b + 1) * T, lanes] = (s_s[b * T : (b + 1) * T, lanes] * inverse).astype(BF)

        by_window(ends, i, run)
        return 0

    lax.fori_loop(0, GROUPS, query_block, 0)


def gather_rows(blocks, vs, gs):
    me = lax.axis_index("ctx")
    for o, block in zip(ORDER, blocks):
        c = lax.rem(me - o + GROUPS, GROUPS)
        vs[pl.ds(pl.multiple_of(c * T, T), T), :] = block[:, 0:D]
        for j in range(GQ):
            gs[c, j * T : (j + 1) * T, :] = block[:, D * (1 + j) : D * (2 + j)]


def gradients(lengths_ref, ks, qs, probs, vs, gs, dk, dv, back, pg_s, db_s):
    factor = 1.0 / math.sqrt(D)
    ends = ends_of(lengths_ref)
    half = 2 * T

    def query_block(i, _):
        def run(blocks):
            start = pl.multiple_of((i - (blocks - 1)) * T, T)
            width = blocks * T
            window = pl.ds(start, width)
            for h in range(2):
                lanes = slice(h * half, (h + 1) * half)
                g = gs[i, lanes, :]
                delta = jnp.zeros((1, half), F32)
                for b in range(blocks):
                    rows = slice(b * T, (b + 1) * T)
                    pg = mm_nt(vs[pl.ds(start + b * T, T), :], g)
                    pg_s[rows, lanes] = pg
                    delta = delta + jnp.sum(probs[i, rows, lanes].astype(F32) * pg, axis=0, keepdims=True)
                for b in range(blocks):
                    rows = slice(b * T, (b + 1) * T)
                    db_s[rows, lanes] = (probs[i, rows, lanes].astype(F32) * (pg_s[rows, lanes] - delta)).astype(BF)
            dv[window, :] += mm(probs[i, 0:width, :], gs[i])
            dk[window, :] += mm(db_s[0:width, :], qs[i])
            dq = lax.dot_general(
                db_s[0:width, :], ks[window, :], (((0,), (0,)), ((), ())), preferred_element_type=F32
            )
            dq = (dq * factor).astype(BF)
            for j in range(GQ):
                back[pl.ds(pl.multiple_of(i * T, T), T), j * D : (j + 1) * D] = dq[j * T : (j + 1) * T, :]

        by_window(ends, i, run)
        return 0

    lax.fori_loop(0, GROUPS, query_block, 0)


def grad_kernel(lengths_ref, ks, qs, probs, place_m, *refs):
    blocks, outs, packed = refs[:GROUPS], refs[GROUPS : 2 * GROUPS], refs[2 * GROUPS]
    dk, dv, vs, gs, back, pg_s, db_s = refs[2 * GROUPS + 1 :]
    me = lax.axis_index("ctx")
    gather_rows(blocks, vs, gs)
    dk[...] = jnp.zeros_like(dk)
    dv[...] = jnp.zeros_like(dv)
    gradients(lengths_ref, ks, qs, probs, vs, gs, dk, dv, back, pg_s, db_s)
    for o, out in zip(ORDER, outs):
        c = lax.rem(me + o, GROUPS)
        out[...] = back[pl.ds(pl.multiple_of(c * T, T), T), 0:BW]
    factor = 1.0 / math.sqrt(D)
    for pair in range(GROUPS // 2):
        parts = []
        for low in range(2):
            rows = pl.ds(pl.multiple_of(source_of(me, 2 * pair + low) * T, T), T)
            parts.append(
                jnp.concatenate(
                    [back[rows, BW : BW + D], (dk[rows, :] * factor).astype(BF), dv[rows, :].astype(BF)], axis=1
                )
            )
        y = jnp.concatenate(parts, axis=0)
        packed[:, 16 * pair : 16 * pair + 16, :] = mm(place_m[pair], y).astype(BF).reshape(S_DP, 16, BW)


def restore_b_kernel(r_ref, early_ref, late_ref, *refs):
    outs, (done, rows) = refs[:GROUPS], refs[GROUPS:]
    done[...] = jnp.zeros_like(done)
    me = lax.axis_index("ctx")
    for pair in range(GROUPS // 2):
        r = r_ref[:, 16 * pair : 16 * pair + 16, :].reshape(2 * SLOTS, BW)
        picks = []
        for low in range(2):
            route_ref, line = (early_ref, late_ref)[pair // 2], 8 * (2 * (pair % 2) + low)
            route_rows = jnp.broadcast_to(route_ref[line : line + 1, :], (T, T))
            _, route_cols, sub_rank = rows_and_columns(route_rows)
            slot = (route_cols * (2 * CAP) + low * CAP + sub_rank).astype(jnp.int32)
            slot = jnp.concatenate([slot] * (2 * SLOTS // T), axis=1)
            picks.append(ones_where(iota((T, 2 * SLOTS), 1) == slot).astype(BF))
        x = mm(jnp.concatenate(picks, axis=0), r).astype(BF)
        for low in range(2):
            c = source_of(me, 2 * pair + low)
            rows[pl.ds(pl.multiple_of(c * T, T), T), :] = x[low * T : (low + 1) * T, :]
    for o, out in zip(ORDER, outs):
        c = lax.rem(me + o, GROUPS)
        out[...] = rows[pl.ds(pl.multiple_of(c * T, T), T), :]


def pack_back_kernel(m_ref, *refs):
    blocks, out = refs[:GROUPS], refs[GROUPS + 1]
    me = lax.axis_index("ctx")
    for o, block in zip(ORDER, blocks):
        g = lax.rem(me - o + GROUPS, GROUPS)
        out[:, pl.ds(pl.multiple_of(g * BW, D), BW)] = mm(m_ref[...], block[...]).astype(BF)


def finish_kernel(routes_ref, r_ref, *refs):
    blocks, (dq, dk, dv) = refs[:GROUPS], refs[GROUPS:]
    me = lax.axis_index("ctx")
    route_rows = jnp.broadcast_to(routes_ref[...].astype(F32), (T, T))
    _, route_cols, sub_rank = rows_and_columns(route_rows)
    slot = (route_cols * CAP + sub_rank).astype(jnp.int32)
    pick = ones_where(iota((T, SLOTS), 1) == jnp.concatenate([slot] * (SLOTS // T), axis=1)).astype(BF)
    for g in range(GROUPS):
        dq[:, g * GQ * D : g * GQ * D + BW] = mm(pick, r_ref[:, g * BW : (g + 1) * BW]).astype(BF)
    for o, block in zip(ORDER, blocks):
        g = lax.rem(me - o + GROUPS, GROUPS)
        dq[:, pl.ds(pl.multiple_of(g * GQ * D + BW, D), D)] = block[:, 0:D]
        dk[:, pl.ds(pl.multiple_of(g * D, D), D)] = block[:, D : 2 * D]
        dv[:, pl.ds(pl.multiple_of(g * D, D), D)] = block[:, 2 * D : 3 * D]


def call(kernel, shapes, args, scratch=(), smem=0, hbm=(), vmem=32, flops=0, aliases=None):
    size = sum(math.prod(s.shape) * s.dtype.itemsize for s in (*shapes, *args))
    specs = [
        pl.BlockSpec(memory_space=pltpu.SMEM if i < smem else pltpu.HBM if i in hbm else pltpu.VMEM)
        for i in range(len(args) + len(shapes))
    ]
    return pl.pallas_call(
        kernel,
        out_shape=list(shapes),
        in_specs=specs[: len(args)],
        out_specs=specs[len(args) :],
        scratch_shapes=list(scratch),
        name=getattr(kernel, "func", kernel).__name__,
        input_output_aliases=aliases or {},
        compiler_params=pltpu.CompilerParams(vmem_limit_bytes=vmem * 1024 * 1024),
        cost_estimate=pl.CostEstimate(flops=flops, bytes_accessed=size, transcendentals=0),
    )(*args)


def shape(*dims, dtype=BF):
    return jax.ShapeDtypeStruct(dims, dtype)


def swap(blocks):
    n = len(blocks)
    return [
        block if o == 0 else lax.ppermute(block, "ctx", [(i, (i + o) % n) for i in range(n)])
        for o, block in zip(ORDER, blocks)
    ]


def exchange(packed):
    return lax.all_to_all(packed, "dp", split_axis=0, concat_axis=0, tiled=True)


def body(queries, key_heads, value_heads, out_grad, routes, doc_lengths):
    q, k, v, g = queries[0], key_heads[0], value_heads[0], out_grad[0]
    *b_blocks, a_packed = call(
        enter_kernel,
        [shape((1 + GQ) * T + 16, D)] * GROUPS + [shape(SLOTS, GROUPS * FW)],
        [routes, k, q, v, g],
        [
            pltpu.VMEM((T, GROUPS * D), BF),
            pltpu.VMEM((T, GROUPS * GQ * D), BF),
            pltpu.VMEM((T, GROUPS * D), BF),
            pltpu.VMEM((T, GROUPS * GQ * D), BF),
            pltpu.VMEM((SLOTS, GROUPS * FW), BF),
            pltpu.VMEM((16, T), BF),
            pltpu.SemaphoreType.DMA((2, GROUPS // 2 + 1)),
            pltpu.SemaphoreType.DMA((GROUPS // 2,)),
            pltpu.SemaphoreType.DMA((GROUPS, 2 + GQ)),
        ],
        hbm=range(1, 6 + GROUPS),
        vmem=60,
        flops=2 * SLOTS * T * GROUPS * FW,
    )
    b_arrived = swap(b_blocks)
    a_arrived = exchange(a_packed.reshape(S_DP, CAP, GROUPS * FW)).reshape(SLOTS, GROUPS * FW)
    place, unpacked, *a_blocks = call(
        unpack_a_kernel,
        [shape(SLOTS, T), shape(8, T, dtype=F32)] + [shape(T, FW)] * GROUPS,
        [a_arrived],
        flops=2 * SLOTS * T * GROUPS * FW,
    )
    a_blocks = swap(a_blocks)

    def pack_b(first_pair, blocks, other, after, aliases):
        return call(
            functools.partial(pack_b_kernel, first_pair),
            [shape(S_DP, GROUPS * CAP, FW), shape(HALF * 8, T, dtype=F32)],
            [*blocks, other, after],
            [
                pltpu.VMEM((HALF * T, FW), BF),
                pltpu.VMEM((S_DP, HALF * CAP, FW), BF),
                pltpu.SemaphoreType.DMA((HALF // 2,)),
            ],
            hbm=(HALF, HALF + 2) if aliases else (HALF + 2,),
            flops=2 * SLOTS * SEQ * FW,
            aliases=aliases,
        )

    b_packed, early_route = pack_b(0, b_arrived[:HALF], routes, routes, {})
    b_packed, late_route = pack_b(HALF // 2, b_arrived[HALF:], b_packed, unpacked, {HALF: 0})
    b_seq = exchange(b_packed)
    place_b, ks, qs, probs = call(
        scores_kernel,
        [
            shape(GROUPS // 2, 2 * SLOTS, 2 * T),
            shape(SEQ, D),
            shape(GROUPS, GQ * T, D),
            shape(GROUPS, WINDOW * T, GQ * T),
        ],
        [doc_lengths, b_seq],
        [pltpu.VMEM((WINDOW * T, GQ * T), F32)],
        smem=1,
        flops=2 * 2 * SLOTS * SEQ * FW + 2 * 24 * T * T * GQ * D,
    )

    *dq_blocks, back_packed = call(
        grad_kernel,
        [shape(T, BW)] * GROUPS + [shape(S_DP, GROUPS * CAP, BW)],
        [doc_lengths, ks, qs, probs, place_b, *a_blocks],
        [
            pltpu.VMEM((SEQ, D), F32),
            pltpu.VMEM((SEQ, D), F32),
            pltpu.VMEM((SEQ, D), BF),
            pltpu.VMEM((GROUPS, GQ * T, D), BF),
            pltpu.VMEM((SEQ, GQ * D), BF),
            pltpu.VMEM((WINDOW * T, GQ * T), F32),
            pltpu.VMEM((WINDOW * T, GQ * T), BF),
        ],
        smem=1,
        flops=4 * 2 * 24 * T * T * GQ * D,
    )
    dq_arrived = swap(dq_blocks)
    back_arrived = exchange(back_packed)
    *rest_blocks, restored = call(
        restore_b_kernel,
        [shape(T, BW)] * GROUPS + [shape(8, T, dtype=F32)],
        [back_arrived, early_route, late_route],
        [pltpu.VMEM((SEQ, BW), BF)],
        flops=2 * 2 * SLOTS * SEQ * BW,
    )
    rest_arrived = swap(rest_blocks)
    (dq_packed,) = call(
        pack_back_kernel,
        [shape(SLOTS, GROUPS * BW)],
        [place, *dq_arrived, restored],
        flops=2 * SLOTS * T * GROUPS * BW,
    )
    dq_back = exchange(dq_packed.reshape(S_DP, CAP, GROUPS * BW)).reshape(SLOTS, GROUPS * BW)
    dq, dk, dv = call(
        finish_kernel,
        [shape(T, GROUPS * GQ * D), shape(T, GROUPS * D), shape(T, GROUPS * D)],
        [routes, dq_back, *rest_arrived],
        flops=2 * SLOTS * T * GROUPS * BW,
    )
    return dq[None], dk[None], dv[None]


def solution(mesh):
    return jax.shard_map(
        body,
        mesh=mesh,
        in_specs=(
            P("dp", "ctx", None),
            P("dp", "ctx", None),
            P("dp", "ctx", None),
            P("dp", "ctx", None),
            P("dp", "ctx"),
            P("dp", None),
        ),
        out_specs=(P("dp", "ctx", None), P("dp", "ctx", None), P("dp", "ctx", None)),
        check_vma=False,
    )
```

```python
import functools
import math

import jax
import jax.numpy as jnp
from jax import lax
from jax.experimental import pallas as pl
from jax.experimental.pallas import tpu as pltpu
from jax.sharding import PartitionSpec as P

GROUPS = 8
GQ = 4
D = 128
T = 128
NDOC = 8
CAP = 8
S_DP = 32
SLOTS = S_DP * CAP
SEQ = GROUPS * T
FW = (1 + GQ) * D
BW = 3 * D
MARK = 1e30
BF = jnp.bfloat16
F32 = jnp.float32
NEG = -1e30
ORDER = (0, 4, 3, 5, 2, 6, 1, 7)
WINDOW = 5


def mm(a, b):
    return jnp.dot(a, b, preferred_element_type=F32)


def mm_nt(a, b):
    return lax.dot_general(a, b, (((1,), (1,)), ((), ())), preferred_element_type=F32)


def iota(shape, dim):
    return lax.broadcasted_iota(jnp.int32, shape, dim)


def ones_where(cond):
    return jnp.where(cond, 1.0, 0.0).astype(F32)


def rows_and_columns(route_rows):
    eye = ones_where(iota((T, T), 0) == iota((T, T), 1)).astype(BF)
    route_cols = mm_nt(eye, route_rows.astype(BF))
    same = route_rows == route_cols
    lane_rank = jnp.sum(ones_where(same & (iota((T, T), 0) < iota((T, T), 1))), axis=0, keepdims=True)
    earlier = ones_where(same & (iota((T, T), 1) < iota((T, T), 0))).astype(BF)
    sub_rank = mm(earlier, jnp.ones((T, T), BF))
    return lane_rank, route_cols, sub_rank


def enter_kernel(routes_ref, k_hbm, q_hbm, v_hbm, g_hbm, *refs):
    outs, packed_hbm = refs[:GROUPS], refs[GROUPS]
    k_ref, q_ref, v_ref, g_ref, packed, route_tile, in_sem, out_sem, stack_sem = refs[GROUPS + 1 :]
    me = lax.axis_index("ctx")
    step = 2
    arriving, leaving = [], []
    for n, g in enumerate(range(0, GROUPS, step)):
        vs, gs = slice(g * D, (g + step) * D), slice(g * GQ * D, (g + step) * GQ * D)
        pair = (
            pltpu.make_async_copy(v_hbm.at[:, vs], v_ref.at[:, vs], in_sem.at[0, n]),
            pltpu.make_async_copy(g_hbm.at[:, gs], g_ref.at[:, gs], in_sem.at[1, n]),
        )
        arriving.append(pair)
        for copy in pair:
            copy.start()
    stacking = (
        pltpu.make_async_copy(q_hbm, q_ref, in_sem.at[0, GROUPS // step]),
        pltpu.make_async_copy(k_hbm, k_ref, in_sem.at[1, GROUPS // step]),
    )
    for copy in stacking:
        copy.start()
    route_tile[...] = jnp.broadcast_to(routes_ref[...].astype(F32), (16, T)).astype(BF)
    route_rows = jnp.broadcast_to(routes_ref[...].astype(F32), (T, T))
    lane_rank, _, _ = rows_and_columns(route_rows)
    slot = (route_rows[0:1, :] * CAP + lane_rank).astype(jnp.int32)
    onehot = ones_where(iota((SLOTS, T), 0) == slot).astype(BF)
    unused = 1.0 - mm(onehot, jnp.ones((T, D), BF))
    for n, pair in enumerate(arriving):
        for copy in pair:
            copy.wait()
        for g in range(n * step, (n + 1) * step):
            values = mm(onehot, v_ref[:, g * D : (g + 1) * D])
            if g == 0:
                values = values + unused * MARK
            packed[:, g * FW : g * FW + D] = values.astype(BF)
            packed[:, g * FW + D : (g + 1) * FW] = mm(onehot, g_ref[:, g * GQ * D : (g + 1) * GQ * D]).astype(BF)
        lanes = slice(n * step * FW, (n + 1) * step * FW)
        leaving.append(pltpu.make_async_copy(packed.at[:, lanes], packed_hbm.at[:, lanes], out_sem.at[n]))
        leaving[-1].start()
        if n == 0:
            for copy in stacking:
                copy.wait()
        for i in range(n * step, (n + 1) * step):
            to = lax.rem(me + ORDER[i], GROUPS)
            parts = [(k_ref.at[:, pl.ds(pl.multiple_of(to * D, D), D)], outs[i].at[0:T, :])]
            for j in range(GQ):
                lanes = pl.ds(pl.multiple_of(to * GQ * D + j * D, D), D)
                parts.append((q_ref.at[:, lanes], outs[i].at[(1 + j) * T : (2 + j) * T, :]))
            parts.append((route_tile, outs[i].at[(1 + GQ) * T : (1 + GQ) * T + 16, :]))
            for m, (source, target) in enumerate(parts):
                leaving.append(pltpu.make_async_copy(source, target, stack_sem.at[i, m]))
                leaving[-1].start()
    for copy in leaving:
        copy.wait()


def unpack_a_kernel(r_ref, m_ref, done, *outs):
    done[...] = jnp.zeros_like(done)
    me = lax.axis_index("ctx")
    flags = ones_where(r_ref[:, 0:D].astype(F32) < 0.5 * MARK)
    lower = ones_where(iota((SLOTS, SLOTS), 1) < iota((SLOTS, SLOTS), 0)).astype(BF)
    flags_b = flags.astype(BF)
    place = mm(lower, flags_b)
    hit = (place == iota((SLOTS, T), 1).astype(F32)) & (flags > 0.5)
    m_ref[...] = ones_where(hit).astype(BF)
    first = ones_where(iota((T, D), 1) == 0).astype(BF)
    flags_t = mm_nt(first, flags_b)
    place_t = mm_nt(flags_t.astype(BF), lower)
    hit_t = (place_t == iota((T, SLOTS), 0).astype(F32)) & (flags_t > 0.5)
    pick = ones_where(hit_t).astype(BF)
    for o, out in zip(ORDER, outs):
        to = lax.rem(me + o, GROUPS)
        out[...] = mm(pick, r_ref[:, pl.ds(pl.multiple_of(to * FW, D), FW)]).astype(BF)


def source_of(me, position):
    return lax.rem(me - ORDER[position] + GROUPS, GROUPS)


HALF = GROUPS // 2


def pack_half(blocks, route_out, rows, out):
    for pair in range(HALF // 2):
        slots = []
        for low in range(2):
            position = 2 * pair + low
            block = blocks[position]
            for j in range(1 + GQ):
                rows[position * T : (position + 1) * T, j * D : (j + 1) * D] = block[j * T : (j + 1) * T, :]
            route_out[8 * position : 8 * position + 8, :] = block[(1 + GQ) * T :, :].astype(F32)[0:8, :]
            route_rows = jnp.broadcast_to(route_out[8 * position : 8 * position + 1, :], (T, T))
            lane_rank, _, _ = rows_and_columns(route_rows)
            slots.append(route_rows[0:1, :] * (2 * CAP) + low * CAP + lane_rank)
        slot = jnp.concatenate(slots, axis=1).astype(jnp.int32)
        onehot = ones_where(iota((2 * SLOTS, 2 * T), 0) == slot).astype(BF)
        unused = 1.0 - mm(onehot, jnp.ones((2 * T, D), BF))
        x = mm(onehot, rows[2 * T * pair : 2 * T * (pair + 1), :])
        lines = slice(16 * pair, 16 * pair + 16)
        out[:, lines, 0:D] = (x[:, 0:D] + unused * MARK).astype(BF).reshape(S_DP, 16, D)
        out[:, lines, D:FW] = x[:, D:FW].astype(BF).reshape(S_DP, 16, FW - D)


def pack_early_kernel(*refs):
    blocks, (out, route_out, rows) = refs[:HALF], refs[HALF:]
    pack_half(blocks, route_out, rows, out)


def pack_late_kernel(*refs):
    blocks, early, (out_hbm, route_out, rows, out, out_sem) = refs[:HALF], refs[HALF], refs[HALF + 2 :]
    lines = HALF * CAP
    sent = [pltpu.make_async_copy(early, out_hbm.at[:, 0:lines, :], out_sem.at[0])]
    sent[0].start()
    pack_half(blocks, route_out, rows, out)
    sent.append(pltpu.make_async_copy(out, out_hbm.at[:, lines : 2 * lines, :], out_sem.at[1]))
    sent[1].start()
    for copy in sent:
        copy.wait()


def ends_of(lengths_ref):
    ends = []
    total = jnp.int32(0)
    for d in range(NDOC):
        total = total + lengths_ref[0, d]
        ends.append(total)
    return ends


def by_window(ends, i, run):
    first_start = jnp.int32(0)
    for end in ends:
        first_start = jnp.where(i * T >= end, end, first_start)
    reach = i - first_start // T + 1
    for blocks in range(1, WINDOW + 1):
        pl.when(reach == blocks)(functools.partial(run, blocks))


def scores_kernel(lengths_ref, r_ref, place_m, ks, qs, probs, s_s):
    two = 2 * SLOTS
    row, col = iota((two, two), 0), iota((two, two), 1)
    lower = ones_where((col < row) & (((row ^ col) & CAP) == 0)).astype(BF)
    slot_low = iota((two, T), 0) & CAP
    first = ones_where(iota((8, D), 1) == 0).astype(BF)
    token = iota((2 * T, two), 0)
    mine = (iota((2 * T, two), 1) & CAP) == (token >> 7) * CAP
    token = (token & (T - 1)).astype(F32)
    me = lax.axis_index("ctx")
    for pair in range(GROUPS // 2):
        r = r_ref[:, 16 * pair : 16 * pair + 16, :].reshape(two, FW)
        flags = ones_where(r[:, 0:D].astype(F32) < 0.5 * MARK)
        flags_b = flags.astype(BF)
        place = mm(lower, flags_b)
        hit = (place == iota((two, T), 1).astype(F32)) & (flags > 0.5)
        for low in range(2):
            place_m[pair, :, low * T : (low + 1) * T] = ones_where(hit & (slot_low == low * CAP)).astype(BF)
        flags_t = mm_nt(first, flags_b)
        place_t = mm_nt(flags_t.astype(BF), lower)
        place_t = jnp.where(flags_t > 0.5, place_t, -1.0)[0:1, :]
        pick = ones_where((place_t == token) & mine).astype(BF)
        x = mm(pick, r).astype(BF)
        for low in range(2):
            c = source_of(me, 2 * pair + low)
            rows = pl.ds(pl.multiple_of(c * T, T), T)
            part = x[low * T : (low + 1) * T, :]
            ks[rows, :] = part[:, 0:D]
            for j in range(GQ):
                qs[c, j * T : (j + 1) * T, :] = part[:, D * (1 + j) : D * (2 + j)]
    ends = ends_of(lengths_ref)
    half = 2 * T
    scale = math.log2(math.e) / math.sqrt(D)

    def query_block(i, _):
        q_pos = i * T + lax.rem(iota((1, half), 1), T)
        doc_start = jnp.zeros((1, half), jnp.int32)
        for end in ends:
            doc_start = jnp.where(q_pos >= end, end, doc_start)

        def run(blocks):
            start = pl.multiple_of((i - (blocks - 1)) * T, T)
            for h in range(2):
                lanes = slice(h * half, (h + 1) * half)
                q = qs[i, lanes, :]
                top = None
                for b in range(blocks):
                    s = mm_nt(ks[pl.ds(start + b * T, T), :], q) * scale
                    k_pos = start + b * T + iota((T, half), 0)
                    keep = k_pos >= doc_start
                    if b == blocks - 1:
                        keep = keep & (k_pos <= q_pos)
                    s = jnp.where(keep, s, NEG)
                    s_s[b * T : (b + 1) * T, lanes] = s
                    high = jnp.max(s, axis=0, keepdims=True)
                    top = high if top is None else jnp.maximum(top, high)
                row_total = jnp.zeros((1, half), F32)
                for b in range(blocks):
                    e = jnp.exp2(s_s[b * T : (b + 1) * T, lanes] - top)
                    s_s[b * T : (b + 1) * T, lanes] = e
                    row_total = row_total + jnp.sum(e, axis=0, keepdims=True)
                inverse = 1.0 / row_total
                for b in range(blocks):
                    probs[i, b * T : (b + 1) * T, lanes] = (s_s[b * T : (b + 1) * T, lanes] * inverse).astype(BF)

        by_window(ends, i, run)
        return 0

    lax.fori_loop(0, GROUPS, query_block, 0)


def gather_rows(blocks, vs, gs):
    me = lax.axis_index("ctx")
    for o, block in zip(ORDER, blocks):
        c = lax.rem(me - o + GROUPS, GROUPS)
        vs[pl.ds(pl.multiple_of(c * T, T), T), :] = block[:, 0:D]
        for j in range(GQ):
            gs[c, j * T : (j + 1) * T, :] = block[:, D * (1 + j) : D * (2 + j)]


def gradients(lengths_ref, ks, qs, probs, vs, gs, dk, dv, back, pg_s, db_s):
    factor = 1.0 / math.sqrt(D)
    ends = ends_of(lengths_ref)
    half = 2 * T

    def query_block(i, _):
        def run(blocks):
            start = pl.multiple_of((i - (blocks - 1)) * T, T)
            width = blocks * T
            window = pl.ds(start, width)
            for h in range(2):
                lanes = slice(h * half, (h + 1) * half)
                g = gs[i, lanes, :]
                delta = jnp.zeros((1, half), F32)
                for b in range(blocks):
                    rows = slice(b * T, (b + 1) * T)
                    pg = mm_nt(vs[pl.ds(start + b * T, T), :], g)
                    pg_s[rows, lanes] = pg
                    delta = delta + jnp.sum(probs[i, rows, lanes].astype(F32) * pg, axis=0, keepdims=True)
                for b in range(blocks):
                    rows = slice(b * T, (b + 1) * T)
                    db_s[rows, lanes] = (probs[i, rows, lanes].astype(F32) * (pg_s[rows, lanes] - delta)).astype(BF)
            dv[window, :] += mm(probs[i, 0:width, :], gs[i])
            dk[window, :] += mm(db_s[0:width, :], qs[i])
            dq = lax.dot_general(
                db_s[0:width, :], ks[window, :], (((0,), (0,)), ((), ())), preferred_element_type=F32
            )
            dq = (dq * factor).astype(BF)
            for j in range(GQ):
                back[pl.ds(pl.multiple_of(i * T, T), T), j * D : (j + 1) * D] = dq[j * T : (j + 1) * T, :]

        by_window(ends, i, run)
        return 0

    lax.fori_loop(0, GROUPS, query_block, 0)


def grad_kernel(lengths_ref, ks, qs, probs, place_m, *refs):
    blocks, outs, packed = refs[:GROUPS], refs[GROUPS : 2 * GROUPS], refs[2 * GROUPS]
    dk, dv, vs, gs, back, pg_s, db_s = refs[2 * GROUPS + 1 :]
    me = lax.axis_index("ctx")
    gather_rows(blocks, vs, gs)
    dk[...] = jnp.zeros_like(dk)
    dv[...] = jnp.zeros_like(dv)
    gradients(lengths_ref, ks, qs, probs, vs, gs, dk, dv, back, pg_s, db_s)
    for o, out in zip(ORDER, outs):
        c = lax.rem(me + o, GROUPS)
        out[...] = back[pl.ds(pl.multiple_of(c * T, T), T), 0:BW]
    factor = 1.0 / math.sqrt(D)
    for pair in range(GROUPS // 2):
        parts = []
        for low in range(2):
            rows = pl.ds(pl.multiple_of(source_of(me, 2 * pair + low) * T, T), T)
            parts.append(
                jnp.concatenate(
                    [back[rows, BW : BW + D], (dk[rows, :] * factor).astype(BF), dv[rows, :].astype(BF)], axis=1
                )
            )
        y = jnp.concatenate(parts, axis=0)
        packed[:, 16 * pair : 16 * pair + 16, :] = mm(place_m[pair], y).astype(BF).reshape(S_DP, 16, BW)


def restore_b_kernel(r_ref, early_ref, late_ref, *refs):
    outs, (done, rows) = refs[:GROUPS], refs[GROUPS:]
    done[...] = jnp.zeros_like(done)
    me = lax.axis_index("ctx")
    for pair in range(GROUPS // 2):
        r = r_ref[:, 16 * pair : 16 * pair + 16, :].reshape(2 * SLOTS, BW)
        picks = []
        for low in range(2):
            route_ref, line = (early_ref, late_ref)[pair // 2], 8 * (2 * (pair % 2) + low)
            route_rows = jnp.broadcast_to(route_ref[line : line + 1, :], (T, T))
            _, route_cols, sub_rank = rows_and_columns(route_rows)
            slot = (route_cols * (2 * CAP) + low * CAP + sub_rank).astype(jnp.int32)
            slot = jnp.concatenate([slot] * (2 * SLOTS // T), axis=1)
            picks.append(ones_where(iota((T, 2 * SLOTS), 1) == slot).astype(BF))
        x = mm(jnp.concatenate(picks, axis=0), r).astype(BF)
        for low in range(2):
            c = source_of(me, 2 * pair + low)
            rows[pl.ds(pl.multiple_of(c * T, T), T), :] = x[low * T : (low + 1) * T, :]
    for o, out in zip(ORDER, outs):
        c = lax.rem(me + o, GROUPS)
        out[...] = rows[pl.ds(pl.multiple_of(c * T, T), T), :]


def pack_back_kernel(m_ref, *refs):
    blocks, out = refs[:GROUPS], refs[GROUPS + 1]
    me = lax.axis_index("ctx")
    for o, block in zip(ORDER, blocks):
        g = lax.rem(me - o + GROUPS, GROUPS)
        out[:, pl.ds(pl.multiple_of(g * BW, D), BW)] = mm(m_ref[...], block[...]).astype(BF)


def finish_kernel(routes_ref, r_ref, *refs):
    blocks, (dq, dk, dv) = refs[:GROUPS], refs[GROUPS:]
    me = lax.axis_index("ctx")
    route_rows = jnp.broadcast_to(routes_ref[...].astype(F32), (T, T))
    _, route_cols, sub_rank = rows_and_columns(route_rows)
    slot = (route_cols * CAP + sub_rank).astype(jnp.int32)
    pick = ones_where(iota((T, SLOTS), 1) == jnp.concatenate([slot] * (SLOTS // T), axis=1)).astype(BF)
    for g in range(GROUPS):
        dq[:, g * GQ * D : g * GQ * D + BW] = mm(pick, r_ref[:, g * BW : (g + 1) * BW]).astype(BF)
    for o, block in zip(ORDER, blocks):
        g = lax.rem(me - o + GROUPS, GROUPS)
        dq[:, pl.ds(pl.multiple_of(g * GQ * D + BW, D), D)] = block[:, 0:D]
        dk[:, pl.ds(pl.multiple_of(g * D, D), D)] = block[:, D : 2 * D]
        dv[:, pl.ds(pl.multiple_of(g * D, D), D)] = block[:, 2 * D : 3 * D]


def call(kernel, shapes, args, scratch=(), smem=0, hbm=(), vmem=32, flops=0):
    size = sum(math.prod(s.shape) * s.dtype.itemsize for s in (*shapes, *args))
    specs = [
        pl.BlockSpec(memory_space=pltpu.SMEM if i < smem else pltpu.HBM if i in hbm else pltpu.VMEM)
        for i in range(len(args) + len(shapes))
    ]
    return pl.pallas_call(
        kernel,
        out_shape=list(shapes),
        in_specs=specs[: len(args)],
        out_specs=specs[len(args) :],
        scratch_shapes=list(scratch),
        name=kernel.__name__,
        compiler_params=pltpu.CompilerParams(vmem_limit_bytes=vmem * 1024 * 1024),
        cost_estimate=pl.CostEstimate(flops=flops, bytes_accessed=size, transcendentals=0),
    )(*args)


def shape(*dims, dtype=BF):
    return jax.ShapeDtypeStruct(dims, dtype)


def swap(blocks):
    n = len(blocks)
    return [
        block if o == 0 else lax.ppermute(block, "ctx", [(i, (i + o) % n) for i in range(n)])
        for o, block in zip(ORDER, blocks)
    ]


def exchange(packed):
    return lax.all_to_all(packed, "dp", split_axis=0, concat_axis=0, tiled=True)


def body(queries, key_heads, value_heads, out_grad, routes, doc_lengths):
    q, k, v, g = queries[0], key_heads[0], value_heads[0], out_grad[0]
    *b_blocks, a_packed = call(
        enter_kernel,
        [shape((1 + GQ) * T + 16, D)] * GROUPS + [shape(SLOTS, GROUPS * FW)],
        [routes, k, q, v, g],
        [
            pltpu.VMEM((T, GROUPS * D), BF),
            pltpu.VMEM((T, GROUPS * GQ * D), BF),
            pltpu.VMEM((T, GROUPS * D), BF),
            pltpu.VMEM((T, GROUPS * GQ * D), BF),
            pltpu.VMEM((SLOTS, GROUPS * FW), BF),
            pltpu.VMEM((16, T), BF),
            pltpu.SemaphoreType.DMA((2, GROUPS // 2 + 1)),
            pltpu.SemaphoreType.DMA((GROUPS // 2,)),
            pltpu.SemaphoreType.DMA((GROUPS, 2 + GQ)),
        ],
        hbm=range(1, 6 + GROUPS),
        vmem=60,
        flops=2 * SLOTS * T * GROUPS * FW,
    )
    b_arrived = swap(b_blocks)
    a_arrived = exchange(a_packed.reshape(S_DP, CAP, GROUPS * FW)).reshape(SLOTS, GROUPS * FW)
    place, unpacked, *a_blocks = call(
        unpack_a_kernel,
        [shape(SLOTS, T), shape(8, T, dtype=F32)] + [shape(T, FW)] * GROUPS,
        [a_arrived],
        flops=2 * SLOTS * T * GROUPS * FW,
    )
    a_blocks = swap(a_blocks)

    half_shape = (S_DP, HALF * CAP, FW)
    early, early_route = call(
        pack_early_kernel,
        [shape(*half_shape), shape(HALF * 8, T, dtype=F32)],
        b_arrived[:HALF],
        [pltpu.VMEM((HALF * T, FW), BF)],
        flops=2 * SLOTS * SEQ * FW,
    )
    b_packed, late_route = call(
        pack_late_kernel,
        [shape(S_DP, GROUPS * CAP, FW), shape(HALF * 8, T, dtype=F32)],
        [*b_arrived[HALF:], early, unpacked],
        [pltpu.VMEM((HALF * T, FW), BF), pltpu.VMEM(half_shape, BF), pltpu.SemaphoreType.DMA((2,))],
        hbm=(HALF + 2,),
        flops=2 * SLOTS * SEQ * FW,
    )
    b_seq = exchange(b_packed)
    place_b, ks, qs, probs = call(
        scores_kernel,
        [
            shape(GROUPS // 2, 2 * SLOTS, 2 * T),
            shape(SEQ, D),
            shape(GROUPS, GQ * T, D),
            shape(GROUPS, WINDOW * T, GQ * T),
        ],
        [doc_lengths, b_seq],
        [pltpu.VMEM((WINDOW * T, GQ * T), F32)],
        smem=1,
        flops=2 * 2 * SLOTS * SEQ * FW + 2 * 24 * T * T * GQ * D,
    )

    *dq_blocks, back_packed = call(
        grad_kernel,
        [shape(T, BW)] * GROUPS + [shape(S_DP, GROUPS * CAP, BW)],
        [doc_lengths, ks, qs, probs, place_b, *a_blocks],
        [
            pltpu.VMEM((SEQ, D), F32),
            pltpu.VMEM((SEQ, D), F32),
            pltpu.VMEM((SEQ, D), BF),
            pltpu.VMEM((GROUPS, GQ * T, D), BF),
            pltpu.VMEM((SEQ, GQ * D), BF),
            pltpu.VMEM((WINDOW * T, GQ * T), F32),
            pltpu.VMEM((WINDOW * T, GQ * T), BF),
        ],
        smem=1,
        flops=4 * 2 * 24 * T * T * GQ * D,
    )
    dq_arrived = swap(dq_blocks)
    back_arrived = exchange(back_packed)
    *rest_blocks, restored = call(
        restore_b_kernel,
        [shape(T, BW)] * GROUPS + [shape(8, T, dtype=F32)],
        [back_arrived, early_route, late_route],
        [pltpu.VMEM((SEQ, BW), BF)],
        flops=2 * 2 * SLOTS * SEQ * BW,
    )
    rest_arrived = swap(rest_blocks)
    (dq_packed,) = call(
        pack_back_kernel,
        [shape(SLOTS, GROUPS * BW)],
        [place, *dq_arrived, restored],
        flops=2 * SLOTS * T * GROUPS * BW,
    )
    dq_back = exchange(dq_packed.reshape(S_DP, CAP, GROUPS * BW)).reshape(SLOTS, GROUPS * BW)
    dq, dk, dv = call(
        finish_kernel,
        [shape(T, GROUPS * GQ * D), shape(T, GROUPS * D), shape(T, GROUPS * D)],
        [routes, dq_back, *rest_arrived],
        flops=2 * SLOTS * T * GROUPS * BW,
    )
    return dq[None], dk[None], dv[None]


def solution(mesh):
    return jax.shard_map(
        body,
        mesh=mesh,
        in_specs=(
            P("dp", "ctx", None),
            P("dp", "ctx", None),
            P("dp", "ctx", None),
            P("dp", "ctx", None),
            P("dp", "ctx"),
            P("dp", None),
        ),
        out_specs=(P("dp", "ctx", None), P("dp", "ctx", None), P("dp", "ctx", None)),
        check_vma=False,
    )
```

```python
import functools
import math

import jax
import jax.numpy as jnp
from jax import lax
from jax.experimental import pallas as pl
from jax.experimental.pallas import tpu as pltpu
from jax.sharding import PartitionSpec as P

GROUPS = 8
GQ = 4
D = 128
T = 128
NDOC = 8
CAP = 8
S_DP = 32
SLOTS = S_DP * CAP
SEQ = GROUPS * T
FW = (1 + GQ) * D
BW = 3 * D
MARK = 1e30
BF = jnp.bfloat16
F32 = jnp.float32
NEG = -1e30
ORDER = (0, 4, 2, 6, 3, 5, 1, 7)
WINDOW = 5


def mm(a, b):
    return jnp.dot(a, b, preferred_element_type=F32)


def mm_nt(a, b):
    return lax.dot_general(a, b, (((1,), (1,)), ((), ())), preferred_element_type=F32)


def iota(shape, dim):
    return lax.broadcasted_iota(jnp.int32, shape, dim)


def ones_where(cond):
    return jnp.where(cond, 1.0, 0.0).astype(F32)


def rows_and_columns(route_rows):
    eye = ones_where(iota((T, T), 0) == iota((T, T), 1)).astype(BF)
    route_cols = mm_nt(eye, route_rows.astype(BF))
    same = route_rows == route_cols
    lane_rank = jnp.sum(ones_where(same & (iota((T, T), 0) < iota((T, T), 1))), axis=0, keepdims=True)
    earlier = ones_where(same & (iota((T, T), 1) < iota((T, T), 0))).astype(BF)
    sub_rank = mm(earlier, jnp.ones((T, T), BF))
    return lane_rank, route_cols, sub_rank


def enter_kernel(routes_ref, k_hbm, q_hbm, v_hbm, g_hbm, *refs):
    outs, packed_hbm = refs[:GROUPS], refs[GROUPS]
    k_ref, q_ref, v_ref, g_ref, packed, route_tile, in_sem, out_sem, stack_sem = refs[GROUPS + 1 :]
    me = lax.axis_index("ctx")
    step = 2
    arriving, leaving = [], []
    for n, g in enumerate(range(0, GROUPS, step)):
        vs, gs = slice(g * D, (g + step) * D), slice(g * GQ * D, (g + step) * GQ * D)
        pair = (
            pltpu.make_async_copy(v_hbm.at[:, vs], v_ref.at[:, vs], in_sem.at[0, n]),
            pltpu.make_async_copy(g_hbm.at[:, gs], g_ref.at[:, gs], in_sem.at[1, n]),
        )
        arriving.append(pair)
        for copy in pair:
            copy.start()
    stacking = (
        pltpu.make_async_copy(q_hbm, q_ref, in_sem.at[0, GROUPS // step]),
        pltpu.make_async_copy(k_hbm, k_ref, in_sem.at[1, GROUPS // step]),
    )
    for copy in stacking:
        copy.start()
    route_tile[...] = jnp.broadcast_to(routes_ref[...].astype(F32), (16, T)).astype(BF)
    route_rows = jnp.broadcast_to(routes_ref[...].astype(F32), (T, T))
    lane_rank, _, _ = rows_and_columns(route_rows)
    slot = (route_rows[0:1, :] * CAP + lane_rank).astype(jnp.int32)
    onehot = ones_where(iota((SLOTS, T), 0) == slot).astype(BF)
    unused = 1.0 - mm(onehot, jnp.ones((T, D), BF))
    for n, pair in enumerate(arriving):
        for copy in pair:
            copy.wait()
        for g in range(n * step, (n + 1) * step):
            values = mm(onehot, v_ref[:, g * D : (g + 1) * D])
            if g == 0:
                values = values + unused * MARK
            packed[:, g * FW : g * FW + D] = values.astype(BF)
            packed[:, g * FW + D : (g + 1) * FW] = mm(onehot, g_ref[:, g * GQ * D : (g + 1) * GQ * D]).astype(BF)
        lanes = slice(n * step * FW, (n + 1) * step * FW)
        leaving.append(pltpu.make_async_copy(packed.at[:, lanes], packed_hbm.at[:, lanes], out_sem.at[n]))
        leaving[-1].start()
        if n == 0:
            for copy in stacking:
                copy.wait()
        for i in range(n * step, (n + 1) * step):
            to = lax.rem(me + ORDER[i], GROUPS)
            parts = [(k_ref.at[:, pl.ds(pl.multiple_of(to * D, D), D)], outs[i].at[0:T, :])]
            for j in range(GQ):
                lanes = pl.ds(pl.multiple_of(to * GQ * D + j * D, D), D)
                parts.append((q_ref.at[:, lanes], outs[i].at[(1 + j) * T : (2 + j) * T, :]))
            parts.append((route_tile, outs[i].at[(1 + GQ) * T : (1 + GQ) * T + 16, :]))
            for m, (source, target) in enumerate(parts):
                leaving.append(pltpu.make_async_copy(source, target, stack_sem.at[i, m]))
                leaving[-1].start()
    for copy in leaving:
        copy.wait()


def unpack_a_kernel(r_ref, m_ref, done, *outs):
    done[...] = jnp.zeros_like(done)
    me = lax.axis_index("ctx")
    flags = ones_where(r_ref[:, 0:D].astype(F32) < 0.5 * MARK)
    lower = ones_where(iota((SLOTS, SLOTS), 1) < iota((SLOTS, SLOTS), 0)).astype(BF)
    flags_b = flags.astype(BF)
    place = mm(lower, flags_b)
    hit = (place == iota((SLOTS, T), 1).astype(F32)) & (flags > 0.5)
    m_ref[...] = ones_where(hit).astype(BF)
    first = ones_where(iota((T, D), 1) == 0).astype(BF)
    flags_t = mm_nt(first, flags_b)
    place_t = mm_nt(flags_t.astype(BF), lower)
    hit_t = (place_t == iota((T, SLOTS), 0).astype(F32)) & (flags_t > 0.5)
    pick = ones_where(hit_t).astype(BF)
    for o, out in zip(ORDER, outs):
        to = lax.rem(me + o, GROUPS)
        out[...] = mm(pick, r_ref[:, pl.ds(pl.multiple_of(to * FW, D), FW)]).astype(BF)


def source_of(me, position):
    return lax.rem(me - ORDER[position] + GROUPS, GROUPS)


HALF = GROUPS // 2


def pack_half(blocks, route_out, rows, out):
    for pair in range(HALF // 2):
        slots = []
        for low in range(2):
            position = 2 * pair + low
            block = blocks[position]
            for j in range(1 + GQ):
                rows[position * T : (position + 1) * T, j * D : (j + 1) * D] = block[j * T : (j + 1) * T, :]
            route_out[8 * position : 8 * position + 8, :] = block[(1 + GQ) * T :, :].astype(F32)[0:8, :]
            route_rows = jnp.broadcast_to(route_out[8 * position : 8 * position + 1, :], (T, T))
            lane_rank, _, _ = rows_and_columns(route_rows)
            slots.append(route_rows[0:1, :] * (2 * CAP) + low * CAP + lane_rank)
        slot = jnp.concatenate(slots, axis=1).astype(jnp.int32)
        onehot = ones_where(iota((2 * SLOTS, 2 * T), 0) == slot).astype(BF)
        unused = 1.0 - mm(onehot, jnp.ones((2 * T, D), BF))
        x = mm(onehot, rows[2 * T * pair : 2 * T * (pair + 1), :])
        lines = slice(16 * pair, 16 * pair + 16)
        out[:, lines, 0:D] = (x[:, 0:D] + unused * MARK).astype(BF).reshape(S_DP, 16, D)
        out[:, lines, D:FW] = x[:, D:FW].astype(BF).reshape(S_DP, 16, FW - D)


def pack_early_kernel(*refs):
    blocks, (out, route_out, rows) = refs[:HALF], refs[HALF:]
    pack_half(blocks, route_out, rows, out)


def pack_late_kernel(*refs):
    blocks, early, (out_hbm, route_out, rows, out, out_sem) = refs[:HALF], refs[HALF], refs[HALF + 2 :]
    lines = HALF * CAP
    sent = [pltpu.make_async_copy(early, out_hbm.at[:, 0:lines, :], out_sem.at[0])]
    sent[0].start()
    pack_half(blocks, route_out, rows, out)
    sent.append(pltpu.make_async_copy(out, out_hbm.at[:, lines : 2 * lines, :], out_sem.at[1]))
    sent[1].start()
    for copy in sent:
        copy.wait()


def ends_of(lengths_ref):
    ends = []
    total = jnp.int32(0)
    for d in range(NDOC):
        total = total + lengths_ref[0, d]
        ends.append(total)
    return ends


def by_window(ends, i, run):
    first_start = jnp.int32(0)
    for end in ends:
        first_start = jnp.where(i * T >= end, end, first_start)
    reach = i - first_start // T + 1
    for blocks in range(1, WINDOW + 1):
        pl.when(reach == blocks)(functools.partial(run, blocks))


def scores_kernel(lengths_ref, r_ref, place_m, ks, qs, probs, s_s):
    two = 2 * SLOTS
    row, col = iota((two, two), 0), iota((two, two), 1)
    lower = ones_where((col < row) & (((row ^ col) & CAP) == 0)).astype(BF)
    slot_low = iota((two, T), 0) & CAP
    first = ones_where(iota((8, D), 1) == 0).astype(BF)
    token = iota((2 * T, two), 0)
    mine = (iota((2 * T, two), 1) & CAP) == (token >> 7) * CAP
    token = (token & (T - 1)).astype(F32)
    me = lax.axis_index("ctx")
    for pair in range(GROUPS // 2):
        r = r_ref[:, 16 * pair : 16 * pair + 16, :].reshape(two, FW)
        flags = ones_where(r[:, 0:D].astype(F32) < 0.5 * MARK)
        flags_b = flags.astype(BF)
        place = mm(lower, flags_b)
        hit = (place == iota((two, T), 1).astype(F32)) & (flags > 0.5)
        for low in range(2):
            place_m[pair, :, low * T : (low + 1) * T] = ones_where(hit & (slot_low == low * CAP)).astype(BF)
        flags_t = mm_nt(first, flags_b)
        place_t = mm_nt(flags_t.astype(BF), lower)
        place_t = jnp.where(flags_t > 0.5, place_t, -1.0)[0:1, :]
        pick = ones_where((place_t == token) & mine).astype(BF)
        x = mm(pick, r).astype(BF)
        for low in range(2):
            c = source_of(me, 2 * pair + low)
            rows = pl.ds(pl.multiple_of(c * T, T), T)
            part = x[low * T : (low + 1) * T, :]
            ks[rows, :] = part[:, 0:D]
            for j in range(GQ):
                qs[c, j * T : (j + 1) * T, :] = part[:, D * (1 + j) : D * (2 + j)]
    ends = ends_of(lengths_ref)
    half = 2 * T
    scale = math.log2(math.e) / math.sqrt(D)

    def query_block(i, _):
        q_pos = i * T + lax.rem(iota((1, half), 1), T)
        doc_start = jnp.zeros((1, half), jnp.int32)
        for end in ends:
            doc_start = jnp.where(q_pos >= end, end, doc_start)

        def run(blocks):
            start = pl.multiple_of((i - (blocks - 1)) * T, T)
            for h in range(2):
                lanes = slice(h * half, (h + 1) * half)
                q = qs[i, lanes, :]
                top = None
                for b in range(blocks):
                    s = mm_nt(ks[pl.ds(start + b * T, T), :], q) * scale
                    k_pos = start + b * T + iota((T, half), 0)
                    keep = k_pos >= doc_start
                    if b == blocks - 1:
                        keep = keep & (k_pos <= q_pos)
                    s = jnp.where(keep, s, NEG)
                    s_s[b * T : (b + 1) * T, lanes] = s
                    high = jnp.max(s, axis=0, keepdims=True)
                    top = high if top is None else jnp.maximum(top, high)
                row_total = jnp.zeros((1, half), F32)
                for b in range(blocks):
                    e = jnp.exp2(s_s[b * T : (b + 1) * T, lanes] - top)
                    s_s[b * T : (b + 1) * T, lanes] = e
                    row_total = row_total + jnp.sum(e, axis=0, keepdims=True)
                inverse = 1.0 / row_total
                for b in range(blocks):
                    probs[i, b * T : (b + 1) * T, lanes] = (s_s[b * T : (b + 1) * T, lanes] * inverse).astype(BF)

        by_window(ends, i, run)
        return 0

    lax.fori_loop(0, GROUPS, query_block, 0)


def gather_rows(blocks, vs, gs):
    me = lax.axis_index("ctx")
    for o, block in zip(ORDER, blocks):
        c = lax.rem(me - o + GROUPS, GROUPS)
        vs[pl.ds(pl.multiple_of(c * T, T), T), :] = block[:, 0:D]
        for j in range(GQ):
            gs[c, j * T : (j + 1) * T, :] = block[:, D * (1 + j) : D * (2 + j)]


def gradients(lengths_ref, ks, qs, probs, vs, gs, dk, dv, back, pg_s, db_s):
    factor = 1.0 / math.sqrt(D)
    ends = ends_of(lengths_ref)
    half = 2 * T

    def query_block(i, _):
        def run(blocks):
            start = pl.multiple_of((i - (blocks - 1)) * T, T)
            width = blocks * T
            window = pl.ds(start, width)
            for h in range(2):
                lanes = slice(h * half, (h + 1) * half)
                g = gs[i, lanes, :]
                delta = jnp.zeros((1, half), F32)
                for b in range(blocks):
                    rows = slice(b * T, (b + 1) * T)
                    pg = mm_nt(vs[pl.ds(start + b * T, T), :], g)
                    pg_s[rows, lanes] = pg
                    delta = delta + jnp.sum(probs[i, rows, lanes].astype(F32) * pg, axis=0, keepdims=True)
                for b in range(blocks):
                    rows = slice(b * T, (b + 1) * T)
                    db_s[rows, lanes] = (probs[i, rows, lanes].astype(F32) * (pg_s[rows, lanes] - delta)).astype(BF)
            dv[window, :] += mm(probs[i, 0:width, :], gs[i])
            dk[window, :] += mm(db_s[0:width, :], qs[i])
            dq = lax.dot_general(
                db_s[0:width, :], ks[window, :], (((0,), (0,)), ((), ())), preferred_element_type=F32
            )
            dq = (dq * factor).astype(BF)
            for j in range(GQ):
                back[pl.ds(pl.multiple_of(i * T, T), T), j * D : (j + 1) * D] = dq[j * T : (j + 1) * T, :]

        by_window(ends, i, run)
        return 0

    lax.fori_loop(0, GROUPS, query_block, 0)


def grad_kernel(lengths_ref, ks, qs, probs, place_m, *refs):
    blocks, outs, packed = refs[:GROUPS], refs[GROUPS : 2 * GROUPS], refs[2 * GROUPS]
    dk, dv, vs, gs, back, pg_s, db_s = refs[2 * GROUPS + 1 :]
    me = lax.axis_index("ctx")
    gather_rows(blocks, vs, gs)
    dk[...] = jnp.zeros_like(dk)
    dv[...] = jnp.zeros_like(dv)
    gradients(lengths_ref, ks, qs, probs, vs, gs, dk, dv, back, pg_s, db_s)
    for o, out in zip(ORDER, outs):
        c = lax.rem(me + o, GROUPS)
        out[...] = back[pl.ds(pl.multiple_of(c * T, T), T), 0:BW]
    factor = 1.0 / math.sqrt(D)
    for pair in range(GROUPS // 2):
        parts = []
        for low in range(2):
            rows = pl.ds(pl.multiple_of(source_of(me, 2 * pair + low) * T, T), T)
            parts.append(
                jnp.concatenate(
                    [back[rows, BW : BW + D], (dk[rows, :] * factor).astype(BF), dv[rows, :].astype(BF)], axis=1
                )
            )
        y = jnp.concatenate(parts, axis=0)
        packed[:, 16 * pair : 16 * pair + 16, :] = mm(place_m[pair], y).astype(BF).reshape(S_DP, 16, BW)


def restore_b_kernel(r_ref, early_ref, late_ref, *refs):
    outs, (done, rows) = refs[:GROUPS], refs[GROUPS:]
    done[...] = jnp.zeros_like(done)
    me = lax.axis_index("ctx")
    for pair in range(GROUPS // 2):
        r = r_ref[:, 16 * pair : 16 * pair + 16, :].reshape(2 * SLOTS, BW)
        picks = []
        for low in range(2):
            route_ref, line = (early_ref, late_ref)[pair // 2], 8 * (2 * (pair % 2) + low)
            route_rows = jnp.broadcast_to(route_ref[line : line + 1, :], (T, T))
            _, route_cols, sub_rank = rows_and_columns(route_rows)
            slot = (route_cols * (2 * CAP) + low * CAP + sub_rank).astype(jnp.int32)
            slot = jnp.concatenate([slot] * (2 * SLOTS // T), axis=1)
            picks.append(ones_where(iota((T, 2 * SLOTS), 1) == slot).astype(BF))
        x = mm(jnp.concatenate(picks, axis=0), r).astype(BF)
        for low in range(2):
            c = source_of(me, 2 * pair + low)
            rows[pl.ds(pl.multiple_of(c * T, T), T), :] = x[low * T : (low + 1) * T, :]
    for o, out in zip(ORDER, outs):
        c = lax.rem(me + o, GROUPS)
        out[...] = rows[pl.ds(pl.multiple_of(c * T, T), T), :]


def pack_back_kernel(m_ref, *refs):
    blocks, out = refs[:GROUPS], refs[GROUPS + 1]
    me = lax.axis_index("ctx")
    for o, block in zip(ORDER, blocks):
        g = lax.rem(me - o + GROUPS, GROUPS)
        out[:, pl.ds(pl.multiple_of(g * BW, D), BW)] = mm(m_ref[...], block[...]).astype(BF)


def finish_kernel(routes_ref, r_ref, *refs):
    blocks, (dq, dk, dv) = refs[:GROUPS], refs[GROUPS:]
    me = lax.axis_index("ctx")
    route_rows = jnp.broadcast_to(routes_ref[...].astype(F32), (T, T))
    _, route_cols, sub_rank = rows_and_columns(route_rows)
    slot = (route_cols * CAP + sub_rank).astype(jnp.int32)
    pick = ones_where(iota((T, SLOTS), 1) == jnp.concatenate([slot] * (SLOTS // T), axis=1)).astype(BF)
    for g in range(GROUPS):
        dq[:, g * GQ * D : g * GQ * D + BW] = mm(pick, r_ref[:, g * BW : (g + 1) * BW]).astype(BF)
    for o, block in zip(ORDER, blocks):
        g = lax.rem(me - o + GROUPS, GROUPS)
        dq[:, pl.ds(pl.multiple_of(g * GQ * D + BW, D), D)] = block[:, 0:D]
        dk[:, pl.ds(pl.multiple_of(g * D, D), D)] = block[:, D : 2 * D]
        dv[:, pl.ds(pl.multiple_of(g * D, D), D)] = block[:, 2 * D : 3 * D]


def call(kernel, shapes, args, scratch=(), smem=0, hbm=(), vmem=32, flops=0):
    size = sum(math.prod(s.shape) * s.dtype.itemsize for s in (*shapes, *args))
    specs = [
        pl.BlockSpec(memory_space=pltpu.SMEM if i < smem else pltpu.HBM if i in hbm else pltpu.VMEM)
        for i in range(len(args) + len(shapes))
    ]
    return pl.pallas_call(
        kernel,
        out_shape=list(shapes),
        in_specs=specs[: len(args)],
        out_specs=specs[len(args) :],
        scratch_shapes=list(scratch),
        name=kernel.__name__,
        compiler_params=pltpu.CompilerParams(vmem_limit_bytes=vmem * 1024 * 1024),
        cost_estimate=pl.CostEstimate(flops=flops, bytes_accessed=size, transcendentals=0),
    )(*args)


def shape(*dims, dtype=BF):
    return jax.ShapeDtypeStruct(dims, dtype)


def swap(blocks):
    n = len(blocks)
    return [
        block if o == 0 else lax.ppermute(block, "ctx", [(i, (i + o) % n) for i in range(n)])
        for o, block in zip(ORDER, blocks)
    ]


def exchange(packed):
    return lax.all_to_all(packed, "dp", split_axis=0, concat_axis=0, tiled=True)


def body(queries, key_heads, value_heads, out_grad, routes, doc_lengths):
    q, k, v, g = queries[0], key_heads[0], value_heads[0], out_grad[0]
    *b_blocks, a_packed = call(
        enter_kernel,
        [shape((1 + GQ) * T + 16, D)] * GROUPS + [shape(SLOTS, GROUPS * FW)],
        [routes, k, q, v, g],
        [
            pltpu.VMEM((T, GROUPS * D), BF),
            pltpu.VMEM((T, GROUPS * GQ * D), BF),
            pltpu.VMEM((T, GROUPS * D), BF),
            pltpu.VMEM((T, GROUPS * GQ * D), BF),
            pltpu.VMEM((SLOTS, GROUPS * FW), BF),
            pltpu.VMEM((16, T), BF),
            pltpu.SemaphoreType.DMA((2, GROUPS // 2 + 1)),
            pltpu.SemaphoreType.DMA((GROUPS // 2,)),
            pltpu.SemaphoreType.DMA((GROUPS, 2 + GQ)),
        ],
        hbm=range(1, 6 + GROUPS),
        vmem=60,
        flops=2 * SLOTS * T * GROUPS * FW,
    )
    b_arrived = swap(b_blocks)
    a_arrived = exchange(a_packed.reshape(S_DP, CAP, GROUPS * FW)).reshape(SLOTS, GROUPS * FW)
    place, unpacked, *a_blocks = call(
        unpack_a_kernel,
        [shape(SLOTS, T), shape(8, T, dtype=F32)] + [shape(T, FW)] * GROUPS,
        [a_arrived],
        flops=2 * SLOTS * T * GROUPS * FW,
    )
    a_blocks = swap(a_blocks)

    half_shape = (S_DP, HALF * CAP, FW)
    early, early_route = call(
        pack_early_kernel,
        [shape(*half_shape), shape(HALF * 8, T, dtype=F32)],
        b_arrived[:HALF],
        [pltpu.VMEM((HALF * T, FW), BF)],
        flops=2 * SLOTS * SEQ * FW,
    )
    b_packed, late_route = call(
        pack_late_kernel,
        [shape(S_DP, GROUPS * CAP, FW), shape(HALF * 8, T, dtype=F32)],
        [*b_arrived[HALF:], early, unpacked],
        [pltpu.VMEM((HALF * T, FW), BF), pltpu.VMEM(half_shape, BF), pltpu.SemaphoreType.DMA((2,))],
        hbm=(HALF + 2,),
        flops=2 * SLOTS * SEQ * FW,
    )
    b_seq = exchange(b_packed)
    place_b, ks, qs, probs = call(
        scores_kernel,
        [
            shape(GROUPS // 2, 2 * SLOTS, 2 * T),
            shape(SEQ, D),
            shape(GROUPS, GQ * T, D),
            shape(GROUPS, WINDOW * T, GQ * T),
        ],
        [doc_lengths, b_seq],
        [pltpu.VMEM((WINDOW * T, GQ * T), F32)],
        smem=1,
        flops=2 * 2 * SLOTS * SEQ * FW + 2 * 24 * T * T * GQ * D,
    )

    *dq_blocks, back_packed = call(
        grad_kernel,
        [shape(T, BW)] * GROUPS + [shape(S_DP, GROUPS * CAP, BW)],
        [doc_lengths, ks, qs, probs, place_b, *a_blocks],
        [
            pltpu.VMEM((SEQ, D), F32),
            pltpu.VMEM((SEQ, D), F32),
            pltpu.VMEM((SEQ, D), BF),
            pltpu.VMEM((GROUPS, GQ * T, D), BF),
            pltpu.VMEM((SEQ, GQ * D), BF),
            pltpu.VMEM((WINDOW * T, GQ * T), F32),
            pltpu.VMEM((WINDOW * T, GQ * T), BF),
        ],
        smem=1,
        flops=4 * 2 * 24 * T * T * GQ * D,
    )
    dq_arrived = swap(dq_blocks)
    back_arrived = exchange(back_packed)
    *rest_blocks, restored = call(
        restore_b_kernel,
        [shape(T, BW)] * GROUPS + [shape(8, T, dtype=F32)],
        [back_arrived, early_route, late_route],
        [pltpu.VMEM((SEQ, BW), BF)],
        flops=2 * 2 * SLOTS * SEQ * BW,
    )
    rest_arrived = swap(rest_blocks)
    (dq_packed,) = call(
        pack_back_kernel,
        [shape(SLOTS, GROUPS * BW)],
        [place, *dq_arrived, restored],
        flops=2 * SLOTS * T * GROUPS * BW,
    )
    dq_back = exchange(dq_packed.reshape(S_DP, CAP, GROUPS * BW)).reshape(SLOTS, GROUPS * BW)
    dq, dk, dv = call(
        finish_kernel,
        [shape(T, GROUPS * GQ * D), shape(T, GROUPS * D), shape(T, GROUPS * D)],
        [routes, dq_back, *rest_arrived],
        flops=2 * SLOTS * T * GROUPS * BW,
    )
    return dq[None], dk[None], dv[None]


def solution(mesh):
    return jax.shard_map(
        body,
        mesh=mesh,
        in_specs=(
            P("dp", "ctx", None),
            P("dp", "ctx", None),
            P("dp", "ctx", None),
            P("dp", "ctx", None),
            P("dp", "ctx"),
            P("dp", None),
        ),
        out_specs=(P("dp", "ctx", None), P("dp", "ctx", None), P("dp", "ctx", None)),
        check_vma=False,
    )
```
